256 devices in a mesh: dp: 32 (over x, z), tensor: 8 (over y, core).
Axes of the slice: x: 4, y: 4, z: 8, core: 2. Of those that a mesh axis runs over, the one named last changes fastest.
Arguments:
- cand_q: bfloat16 [16384, 4096], P('dp', 'tensor'), may hold values from -6 to 6
- cand_k: bfloat16 [16384, 1024], P('dp', 'tensor'), may hold values from -6 to 6
- cand_v: bfloat16 [16384, 1024], P('dp', 'tensor'), may hold values from -6 to 6
- prompt_k: bfloat16 [32768, 1024], P('dp', 'tensor'), may hold values from -6 to 6
- prompt_v: bfloat16 [32768, 1024], P('dp', 'tensor'), may hold values from -6 to 6
- cand_group: int32 [512], P('dp'), may hold values from 0 to 31, as said below
- cand_len: int32 [512], P('dp'), may hold values from 8 to 32, as said below
- boundaries: int32 [512, 4], P('dp'), may hold values from 0 to 31, as said below
- residual: bfloat16 [16384, 8192], P(('dp', 'tensor')), may hold values from -3 to 3
- out_weight: bfloat16 [4096, 8192], P('tensor'), may hold values from -0.5 to 0.5
- head_weight: float32 [8192], replicated, may hold values from -0.0625 to 0.0625
Outputs:
- hidden_out: bfloat16 [16384, 8192], P(('dp', 'tensor'))
- rewards: float32 [512, 4], P(('dp', 'tensor'))
The draws below stay inside these ranges and needn't reach their ends.
Inputs may be any that keep to these rules, and one draw needn't show every extreme that they name: `cand_group`: the candidates of one index of dp name each problem at most 2 times; in every draw one problem is named exactly 2 times by the candidates of every index of dp. `cand_len`: some candidate has length 32. A candidate's boundaries never fall and lie below its length; the last is its length minus one.
All inputs are finite; a program needn't handle non-finite values.
Results may differ from the reference program's by a relative error of at most 0.017.
Values may be sent and summed in bfloat16 or wider, within the bound.
A program may use at most 128 MiB of HBM per device.

```python
import math
import jax
import jax.numpy as jnp
from jax import lax

D = 8192
HEADS = 32
KVH = 8
HD = 128
P_SIZE = 1024
L = 32
C_DEV = 16
PAIR = 2
NB = 4
PROBLEMS = 32
CANDS = 512
TOKENS = 16384
N_TENSOR = 8


def length_and_steps(key):
    key = jax.random.fold_in(key, 102)
    len_key, full_key, mark_key = jax.random.split(key, 3)
    lengths = jax.random.randint(len_key, (CANDS,), L // 4, L + 1)
    full_one = jax.random.randint(full_key, (), 0, CANDS)
    lengths = jnp.where(jnp.arange(CANDS) == full_one, L, lengths)
    step_marks = jax.random.randint(mark_key, (CANDS, NB - 1), 0, L) % lengths[:, None]
    step_marks = jnp.sort(step_marks, axis=1)
    step_marks = jnp.concatenate([step_marks, (lengths - 1)[:, None]], axis=1)
    return (lengths.astype(jnp.int32), step_marks.astype(jnp.int32))


def draw_cand_q(key, part):
    key = jax.random.fold_in(key, 11)
    drawn = jax.random.truncated_normal(key, -6.0, 6.0, (TOKENS, HEADS * HD), jnp.float32)
    return drawn.astype(jnp.bfloat16)


def draw_cand_k(key, part):
    key = jax.random.fold_in(key, 12)
    drawn = 1.5 * jax.random.truncated_normal(key, -4.0, 4.0, (TOKENS, KVH * HD), jnp.float32)
    return drawn.astype(jnp.bfloat16)


def draw_prompt_k(key, part):
    key = jax.random.fold_in(key, 13)
    drawn = jax.random.truncated_normal(key, -6.0, 6.0, (PROBLEMS * P_SIZE, KVH * HD), jnp.float32)
    return drawn.astype(jnp.bfloat16)


def draw_cand_group(key, part):
    key = jax.random.fold_in(key, 21)
    hot_key, heat_key, jitter_key, order_key = jax.random.split(key, 4)
    slot_total = PROBLEMS * PAIR
    slot_owner = jnp.arange(slot_total, dtype=jnp.int32) // PAIR
    hot_owner = jax.random.randint(hot_key, (), 0, PROBLEMS)
    owner_heat = jax.random.randint(heat_key, (PROBLEMS,), 0, 4)
    jitter = jax.random.randint(jitter_key, (PROBLEMS, slot_total), 0, 1 << 18)
    priority = owner_heat[slot_owner][None, :] * (1 << 16) + jitter + (slot_owner == hot_owner).astype(jnp.int32)[None, :] * (1 << 20)
    priority = priority * slot_total + jnp.arange(slot_total, dtype=jnp.int32)[None, :]
    _, picked = lax.top_k(priority, C_DEV)
    problem_of = picked // PAIR
    shuffle = jax.random.randint(order_key, (PROBLEMS, C_DEV), 0, 1 << 20) * C_DEV + jnp.arange(C_DEV, dtype=jnp.int32)[None, :]
    shuffle_order = jnp.argsort(shuffle, axis=1)
    problem_of = jnp.take_along_axis(problem_of, shuffle_order, axis=1)
    return problem_of.reshape(CANDS).astype(jnp.int32)


def draw_cand_len(key, part):
    lengths, step_marks = length_and_steps(key)
    return lengths


def draw_boundaries(key, part):
    lengths, step_marks = length_and_steps(key)
    return step_marks


def levels(key, dims, shards, least, high):
    level, own = 1.0, jax.random.fold_in(key, 6)
    for axis_at, shards_of in shards:
        draws = jnp.exp(jax.random.uniform(jax.random.fold_in(own, axis_at), (shards_of,), jnp.float32, least / len(shards), high / len(shards)))
        level = level * jnp.repeat(draws, dims[axis_at] // shards_of).reshape([-1 if axis == axis_at else 1 for axis in range(len(dims))])
    return level


def noise(own_key, extent, scale, bound, cuts=(), kind=jnp.bfloat16):
    factor_of = levels(own_key, extent, cuts, -0.22, 0.18) if cuts else 1.0
    values = jax.random.normal(own_key, extent, jnp.float32) * scale * factor_of
    return jnp.minimum(jnp.maximum(values, -bound), bound).astype(kind)


def setup_inputs(seed: int = 0) -> dict:
    seeds = jax.random.split(jax.random.key(seed), 12)
    return {
        "cand_q": draw_cand_q(jax.random.fold_in(seeds[11], 71), 0),
        "cand_k": draw_cand_k(jax.random.fold_in(seeds[11], 71), 0),
        "cand_v": noise(seeds[2], (TOKENS, KVH * HD), 1.0, 6.0, ((0, 32), (1, 8))),
        "prompt_k": draw_prompt_k(jax.random.fold_in(seeds[11], 71), 0),
        "prompt_v": noise(seeds[4], (PROBLEMS * P_SIZE, KVH * HD), 1.0, 6.0, ((0, 32), (1, 8))),
        "cand_group": draw_cand_group(jax.random.fold_in(seeds[11], 71), 0),
        "cand_len": draw_cand_len(jax.random.fold_in(seeds[11], 71), 0),
        "boundaries": draw_boundaries(jax.random.fold_in(seeds[11], 71), 0),
        "residual": noise(seeds[8], (TOKENS, D), 0.5, 3.0, ((0, 256),)),
        "out_weight": noise(seeds[9], (HEADS * HD, D), HD ** -0.5, 0.5, ((0, 8),)),
        "head_weight": noise(seeds[10], (D,), D ** -0.5, 0.0625, (), jnp.float32),
    }


def soften(scores, value_rows, out_spec):
    highest = lax.optimization_barrier(jnp.max(scores, axis=-1, keepdims=True))
    raised = jnp.exp(scores - highest)
    summed_exp = lax.optimization_barrier(jnp.sum(raised, axis=-1, keepdims=True))
    shares = (raised / summed_exp).astype(jnp.bfloat16)
    mixed = jnp.einsum(out_spec, shares.astype(jnp.float32), value_rows.astype(jnp.float32))
    return (mixed, (highest + jnp.log(summed_exp))[..., 0])

def merge_parts(prefix_out, prefix_lse, suffix_out, suffix_lse):
    largest = jnp.maximum(prefix_lse, suffix_lse)
    prefix_weight = jnp.exp(prefix_lse - largest)[..., None]
    suffix_weight = jnp.exp(suffix_lse - largest)[..., None]
    joined = prefix_weight * prefix_out + suffix_weight * suffix_out
    return (joined / (prefix_weight + suffix_weight)).astype(jnp.bfloat16)

def reference(cand_q, cand_k, cand_v, prompt_k, prompt_v, cand_group, cand_len, boundaries, residual, out_weight, head_weight):
    group_ratio = HEADS // KVH
    score_scale = 1.0 / math.sqrt(HD)
    queries = cand_q.reshape(CANDS, L, KVH, group_ratio, HD)
    key_rows = cand_k.reshape(CANDS, L, KVH, HD)
    value_rows = cand_v.reshape(CANDS, L, KVH, HD)
    all_keys = prompt_k.reshape(PROBLEMS, P_SIZE, KVH, HD)
    all_values = prompt_v.reshape(PROBLEMS, P_SIZE, KVH, HD)
    causal = (jnp.arange(L)[:, None] >= jnp.arange(L)[None, :])[:, None, None, :]

    def attend(candidate):
        query_rows, own_keys, own_values, problem = candidate
        query_rows = query_rows.astype(jnp.float32)
        prompt_keys = lax.dynamic_index_in_dim(all_keys, problem, 0, keepdims=False).astype(jnp.float32)
        prompt_values = lax.dynamic_index_in_dim(all_values, problem, 0, keepdims=False)
        prefix_scores = jnp.einsum('lkrd,pkd->lkrp', query_rows, prompt_keys) * score_scale
        prefix_out, prefix_lse = soften(prefix_scores, prompt_values, 'lkrp,pkd->lkrd')
        prefix_out = lax.optimization_barrier(prefix_out.astype(jnp.bfloat16)).astype(jnp.float32)
        suffix_scores = jnp.einsum('lkrd,mkd->lkrm', query_rows, own_keys.astype(jnp.float32)) * score_scale
        suffix_scores = jnp.where(causal, suffix_scores, -1e+30)
        suffix_out, suffix_lse = soften(suffix_scores, own_values, 'lkrm,mkd->lkrd')
        return merge_parts(prefix_out, prefix_lse, suffix_out, suffix_lse)
    attention = lax.map(attend, (queries, key_rows, value_rows, cand_group)).reshape(TOKENS, HEADS * HD)
    head_width = HEADS * HD // N_TENSOR
    positions = jnp.arange(TOKENS, dtype=jnp.int32) % L
    is_live = positions < jnp.repeat(cand_len, L, total_repeat_length=TOKENS)

    def project(block):
        attn_rows, input_rows, live_rows = block
        combined = input_rows.astype(jnp.float32)
        for column_group in range(N_TENSOR):
            first_column = column_group * head_width
            partial_sum = jnp.dot(attn_rows[:, first_column:first_column + head_width], out_weight[first_column:first_column + head_width], preferred_element_type=jnp.float32)
            combined = combined + lax.optimization_barrier(partial_sum.astype(jnp.bfloat16)).astype(jnp.float32)
        return jnp.where(live_rows[:, None], combined, 0.0).astype(jnp.bfloat16)
    hidden_out = lax.map(project, (attention.reshape(PROBLEMS, C_DEV * L, HEADS * HD), residual.reshape(PROBLEMS, C_DEV * L, D), is_live.reshape(PROBLEMS, C_DEV * L))).reshape(TOKENS, D)
    row_index = (jnp.arange(CANDS, dtype=jnp.int32)[:, None] * L + boundaries.astype(jnp.int32)).reshape(CANDS * NB).astype(jnp.int32)
    picked = jnp.take(hidden_out, row_index, axis=0).astype(jnp.float32)
    normed = picked * lax.rsqrt(lax.optimization_barrier(jnp.mean(picked * picked, axis=-1, keepdims=True)) + 1e-06)
    logits = lax.optimization_barrier(jnp.sum(normed * head_weight[None, :], axis=-1))
    rewards = jax.nn.sigmoid(logits).reshape(CANDS, NB)
    return (hidden_out, rewards)
```

```python
import functools
import math

import jax
import jax.numpy as jnp
from jax import lax
from jax.experimental import pallas as pl
from jax.experimental.pallas import tpu as pltpu
from jax.sharding import PartitionSpec as P

HD = 128
P_SIZE = 1024
L = 32
C = 16
PAIR = 2
R = 4
XN, ZN, YN = 4, 8, 4
D = 8192
SCALE = 1.0 / math.sqrt(HD)
LOG2E = 1.4426950408889634
TILE = 1024
TILES = D // TILE
F32 = jnp.float32
BF16 = jnp.bfloat16
VMEM_LIMIT = 56 * 1024 * 1024


def remote(src, dst, send_sem, recv_sem, device):
    return pltpu.make_async_remote_copy(
        src_ref=src,
        dst_ref=dst,
        send_sem=send_sem,
        recv_sem=recv_sem,
        device_id=device,
        device_id_type=pl.DeviceIdType.MESH,
    )


def barrier_with(devices):
    barrier = pltpu.get_barrier_semaphore()
    for device in devices:
        pl.semaphore_signal(
            barrier, inc=1, device_id=device, device_id_type=pl.DeviceIdType.MESH
        )
    pl.semaphore_wait(barrier, len(devices))


def rows_of(block):
    return jnp.concatenate([block[:, r * HD : (r + 1) * HD] for r in range(R)], axis=0)


def with_ones(values):
    return jnp.concatenate([values, jnp.ones(values.shape, values.dtype)], axis=1)


def soften(scores, value_rows):
    highest = jnp.max(scores, axis=-1, keepdims=True)
    raised = jnp.exp2((scores - highest) * (SCALE * LOG2E)).astype(BF16)
    mixed = jnp.dot(raised, with_ones(value_rows), preferred_element_type=F32)
    summed = mixed[:, HD:]
    return mixed[:, :HD] / summed, highest * SCALE + jnp.log(summed)


def scores_of(queries, keys):
    return lax.dot_general(
        queries, keys, (((1,), (1,)), ((), ())), preferred_element_type=F32
    )


def attend_kernel(
    group_s, q_in, ck, cv, pk, pv, attn,
    qbuf, kbuf, vbuf, tabv, tabs, res, lsb, rel_r, rel_l, sfo, sfl, slot_s,
    loc_sem, tab_ss, tab_rs, q_ss, q_rs, k_ss, k_rs, v_ss, v_rs,
    ret_ss, ret_rs, fwd_ss, fwd_rs, lse_ss, lse_rs,
):
    dp = lax.axis_index("dp")
    x, z = dp // ZN, dp % ZN
    xl = {"dp": ((x + XN - 1) % XN) * ZN + z}
    xr = {"dp": ((x + 1) % XN) * ZN + z}
    xx = {"dp": ((x + 2) % XN) * ZN + z}
    zl = {"dp": x * ZN + (z + ZN - 1) % ZN}
    zr = {"dp": x * ZN + (z + 1) % ZN}

    own_k = pltpu.make_async_copy(pk, kbuf.at[0], loc_sem.at[0])
    own_v = pltpu.make_async_copy(pv, vbuf.at[0], loc_sem.at[1])
    own_q = pltpu.make_async_copy(q_in, qbuf.at[pl.ds(0, C)], loc_sem.at[2])
    own_q.start()
    own_k.start()
    own_v.start()

    groups = [group_s[c] for c in range(C)]
    lane = lax.broadcasted_iota(jnp.int32, (8, 128), 1)
    table = jnp.zeros((8, 128), jnp.int32)
    for c in range(C):
        slot = jnp.int32(0)
        for e in range(c):
            slot = slot + jnp.where(groups[e] == groups[c], 1, 0)
        slot = jnp.minimum(slot, PAIR - 1)
        table = jnp.where(lane == groups[c] * PAIR + slot, c, table)
        away = (groups[c] // ZN - x + XN) % XN
        region = jnp.where(away == 0, 0, jnp.where(away == 3, 4, jnp.where(away == 1, 5, 6)))
        back = (z - groups[c] % ZN + ZN) % ZN
        order = jnp.where(back == 0, 0, jnp.where(back <= 4, 2 * back - 1, 2 * (ZN - back)))
        slot_s[c] = region * C + order * PAIR + slot
    tabv[0] = table

    barrier_with([zl, zr, xl, xr, xx])

    def k_to(n, src, device):
        return remote(src, kbuf.at[n], k_ss.at[n], k_rs.at[n], device)

    def v_to(n, src, device):
        return remote(src, vbuf.at[n], v_ss.at[n], v_rs.at[n], device)

    k_to(1, pk, zr).start()
    k_to(2, pk, zl).start()
    half = C // 2
    lo, hi = pl.ds(0, half), pl.ds(half, half)

    def q_copy(i, src, region, part, device):
        return remote(
            src, qbuf.at[pl.ds(region * C + part * half, half)], q_ss.at[i], q_rs.at[i], device
        )

    q_copies = [
        q_copy(0, q_in.at[lo], 1, 0, xr),
        q_copy(1, q_in.at[hi], 2, 1, xl),
        q_copy(2, q_in.at[hi], 1, 1, xr),
        q_copy(3, q_in.at[lo], 2, 0, xl),
        q_copy(4, qbuf.at[pl.ds(1 * C, half)], 3, 0, xr),
        q_copy(5, qbuf.at[pl.ds(2 * C + half, half)], 3, 1, xl),
    ]
    q_copies[0].start()
    q_copies[1].start()
    v_to(1, pv, zr).start()
    v_to(2, pv, zl).start()
    tab_copies = [
        remote(tabv.at[0], tabv.at[1], tab_ss.at[0], tab_rs.at[0], xr),
        remote(tabv.at[0], tabv.at[2], tab_ss.at[1], tab_rs.at[1], xl),
        remote(tabv.at[0], tabv.at[3], tab_ss.at[2], tab_rs.at[2], xx),
    ]
    for copy in tab_copies:
        copy.start()
    q_copies[2].start()
    q_copies[3].start()

    own_q.wait()
    row = lax.broadcasted_iota(jnp.int32, (4 * R * L, 4 * L), 0)
    col = lax.broadcasted_iota(jnp.int32, (4 * R * L, 4 * L), 1)
    allowed = (row // (R * L) == col // L) & (col % L <= row % L)

    def suffix(g, carry):
        queries = jnp.concatenate([rows_of(qbuf[g * 4 + k]) for k in range(4)], axis=0)
        keys = ck[pl.ds(g * 4 * L, 4 * L), :]
        scores = jnp.where(allowed, scores_of(queries, keys), -1e30)
        mixed, lse = soften(scores, cv[pl.ds(g * 4 * L, 4 * L), :])
        for k in range(4):
            sfo[g * 4 + k] = mixed[k * R * L : (k + 1) * R * L]
            sfl[g * 4 + k] = lse[k * R * L : (k + 1) * R * L]
        return carry

    lax.fori_loop(0, C // 4, suffix, 0)

    q_copies[0].wait_recv()
    q_copies[4].start()
    q_copies[1].wait_recv()
    q_copies[5].start()
    own_k.wait()
    own_v.wait()
    for n, device in ((1, zr), (2, zl)):
        k_to(n, kbuf.at[n], device).wait_recv()
        k_to(n + 2, kbuf.at[n], device).start()
    for n, device in ((1, zr), (2, zl)):
        v_to(n, vbuf.at[n], device).wait_recv()
        v_to(n + 2, vbuf.at[n], device).start()
    for copy in tab_copies:
        copy.wait_recv()
    to_smem = pltpu.make_async_copy(tabv, tabs, loc_sem.at[3])
    to_smem.start()
    for i in (2, 3, 4, 5):
        q_copies[i].wait_recv()
    to_smem.wait()

    eye = lax.broadcasted_iota(jnp.int32, (HD, HD), 0) == lax.broadcasted_iota(
        jnp.int32, (HD, HD), 1
    )

    def pair_at(region, n):
        return pl.ds(region * C + n * PAIR, PAIR)

    def one_at(region, n, u):
        return pl.ds(region * C + n * PAIR + u, 1)

    def returns(n):
        return (
            remote(res.at[pair_at(1, n)], res.at[pair_at(5, n)], ret_ss.at[0, n], ret_rs.at[0, n], xl),
            remote(res.at[pair_at(2, n)], res.at[pair_at(4, n)], ret_ss.at[1, n], ret_rs.at[1, n], xr),
            remote(res.at[one_at(3, n, 0)], rel_r.at[pl.ds(n, 1)], ret_ss.at[2, n], ret_rs.at[2, n], xr),
            remote(res.at[one_at(3, n, 1)], rel_l.at[pl.ds(n, 1)], ret_ss.at[3, n], ret_rs.at[3, n], xl),
        )

    def relays(n):
        return (
            remote(rel_r.at[pl.ds(n, 1)], res.at[one_at(6, n, 0)], fwd_ss.at[0, n], fwd_rs.at[0, n], xr),
            remote(rel_l.at[pl.ds(n, 1)], res.at[one_at(6, n, 1)], fwd_ss.at[1, n], fwd_rs.at[1, n], xl),
        )

    def relay(n):
        _, _, right, left = returns(n)
        on_right, on_left = relays(n)
        right.wait_recv()
        on_right.start()
        left.wait_recv()
        on_left.start()

    def step(n, carry):
        @pl.when(n == 2)
        def _():
            for m, device in ((3, zr), (4, zl)):
                k_to(m, kbuf.at[m], device).wait_recv()
                k_to(m + 2, kbuf.at[m], device).start()

        @pl.when(n == 3)
        def _():
            for m, device in ((3, zr), (4, zl)):
                v_to(m, vbuf.at[m], device).wait_recv()
                v_to(m + 2, vbuf.at[m], device).start()

        @pl.when(n == 5)
        def _():
            k_to(5, kbuf.at[5], zr).wait_recv()
            k_to(7, kbuf.at[5], zr).start()
            k_to(6, kbuf.at[6], zl).wait_recv()
            v_to(6, vbuf.at[6], zl).wait_recv()
            v_to(7, vbuf.at[6], zl).start()
            v_to(5, vbuf.at[5], zr).wait_recv()

        @pl.when(n == 7)
        def _():
            k_to(7, kbuf.at[5], zr).wait_recv()
            v_to(7, vbuf.at[6], zl).wait_recv()

        owner_z = (z + (1 - 2 * (n % 2)) * ((n + 1) // 2) + ZN) % ZN
        base = (x * ZN + owner_z) * PAIR

        def source(s, inner):
            queries = jnp.concatenate(
                [rows_of(qbuf[s * C + tabs[s, 0, base + u]]) for u in range(PAIR)], axis=0
            )
            mixed, lse = soften(scores_of(queries, kbuf[n]), vbuf[n])
            mixed = mixed.astype(BF16)
            for u in range(PAIR):
                at = s * C + n * PAIR + u
                for r in range(R):
                    first = (u * R + r) * L
                    res[at, :, r * HD : (r + 1) * HD] = mixed[first : first + L]
                lsb[at] = jnp.sum(
                    jnp.where(eye, lse[u * HD : (u + 1) * HD], 0.0), axis=0, keepdims=True
                )
            return inner

        lax.fori_loop(0, XN, source, 0)
        for copy in returns(n):
            copy.start()

        @pl.when(n >= 2)
        def _():
            relay(n - 2)

        return carry

    lax.fori_loop(0, ZN, step, 0)
    lse_copies = [
        remote(lsb.at[pl.ds(1 * C, C)], lsb.at[pl.ds(5 * C, C)], lse_ss.at[0], lse_rs.at[0], xl),
        remote(lsb.at[pl.ds(2 * C, C)], lsb.at[pl.ds(4 * C, C)], lse_ss.at[1], lse_rs.at[1], xr),
        remote(lsb.at[pl.ds(3 * C, C)], lsb.at[pl.ds(6 * C, C)], lse_ss.at[2], lse_rs.at[2], xx),
    ]
    for copy in lse_copies:
        copy.start()
    relay(ZN - 2)
    relay(ZN - 1)

    def arrived(n, carry):
        from_xl, from_xr, _, _ = returns(n)
        from_xl.wait_recv()
        from_xr.wait_recv()
        for copy in relays(n):
            copy.wait_recv()
        return carry

    lax.fori_loop(0, ZN, arrived, 0)
    for copy in lse_copies:
        copy.wait_recv()

    def merge(c, carry):
        at = slot_s[c]
        prefix = rows_of(res[at]).astype(F32)
        prefix_lse = jnp.sum(jnp.where(eye, lsb[at], 0.0), axis=1, keepdims=True)
        suffix_lse = sfl[c]
        largest = jnp.maximum(prefix_lse, suffix_lse)
        a = jnp.exp(prefix_lse - largest)
        b = jnp.exp(suffix_lse - largest)
        joined = ((a * prefix + b * sfo[c]) / (a + b)).astype(BF16)
        for r in range(R):
            attn[c, :, r * HD : (r + 1) * HD] = joined[r * L : (r + 1) * L]
        return carry

    lax.fori_loop(0, C, merge, 0)

    def sent(n, carry):
        for copy in returns(n) + relays(n):
            copy.wait_send()
        return carry

    lax.fori_loop(0, ZN, sent, 0)
    for copy in lse_copies + q_copies + tab_copies:
        copy.wait_send()
    for n in range(1, ZN):
        k_to(n, kbuf.at[0], zr).wait_send()
        v_to(n, vbuf.at[0], zr).wait_send()


def attend(group, q, ck, cv, pk, pv):
    dma = pltpu.SemaphoreType.DMA
    any_space = pl.BlockSpec(memory_space=pl.ANY)
    vmem = pl.BlockSpec(memory_space=pltpu.VMEM)
    smem = pl.BlockSpec(memory_space=pltpu.SMEM)
    return pl.pallas_call(
        attend_kernel,
        out_shape=jax.ShapeDtypeStruct((C, L, R * HD), BF16),
        in_specs=[smem, any_space, vmem, vmem, any_space, any_space],
        out_specs=vmem,
        scratch_shapes=[
            pltpu.VMEM((XN * C, L, R * HD), BF16),
            pltpu.VMEM((ZN, P_SIZE, HD), BF16),
            pltpu.VMEM((ZN, P_SIZE, HD), BF16),
            pltpu.VMEM((XN, 8, 128), jnp.int32),
            pltpu.SMEM((XN, 8, 128), jnp.int32),
            pltpu.VMEM((7 * C, L, R * HD), BF16),
            pltpu.VMEM((7 * C, 1, HD), F32),
            pltpu.VMEM((ZN, L, R * HD), BF16),
            pltpu.VMEM((ZN, L, R * HD), BF16),
            pltpu.VMEM((C, R * L, HD), F32),
            pltpu.VMEM((C, R * L, HD), F32),
            pltpu.SMEM((C,), jnp.int32),
            dma((4,)), dma((3,)), dma((3,)), dma((6,)), dma((6,)),
            dma((ZN,)), dma((ZN,)), dma((ZN,)), dma((ZN,)),
            dma((4, ZN)), dma((4, ZN)), dma((2, ZN)), dma((2, ZN)), dma((3,)), dma((3,)),
        ],
        compiler_params=pltpu.CompilerParams(
            collective_id=0, has_side_effects=True, vmem_limit_bytes=VMEM_LIMIT
        ),
        cost_estimate=pl.CostEstimate(
            flops=2 * 2 * 64 * 128 * P_SIZE * HD, bytes_accessed=8 << 20, transcendentals=8 << 20
        ),
    )(group, q, ck, cv, pk, pv)


def project_kernel(
    len_s, mark_s, attn, weight, residual, head_w, hidden, rewards,
    wbuf, send_a, recv_a, own, far_r, far_l, near_l, near_r, squares, dots,
    w_sem, a_ss, a_rs, far_ss, far_rs, now_ss, now_rs, late_ss, late_rs,
):
    t = lax.axis_index("tensor")
    y, core = t // 2, t % 2
    sibling = {"tensor": y * 2 + 1 - core}
    yr_at, yl_at, far_at = (y + 1) % YN, (y + YN - 1) % YN, (y + 2) % YN
    yr = {"tensor": yr_at * 2 + core}
    yl = {"tensor": yl_at * 2 + core}
    rows = C * L // (2 * YN)
    half = rows // 2
    lo, hi = pl.ds(0, half), pl.ds(half, half)

    def w_copy(i):
        return pltpu.make_async_copy(
            weight.at[:, pl.ds(pl.multiple_of(i * TILE, TILE), TILE)], wbuf.at[i], w_sem.at[i]
        )

    for i in range(TILES):
        w_copy(i).start()
    squares[...] = jnp.zeros_like(squares)
    dots[...] = jnp.zeros_like(dots)
    barrier_with([sibling, yl, yr])

    def a_copy(i):
        return remote(send_a.at[i], recv_a.at[i], a_ss.at[i], a_rs.at[i], sibling)

    def far_copies(i):
        return (
            remote(own.at[i, far_at, lo], far_r.at[i], far_ss.at[0, i], far_rs.at[0, i], yr),
            remote(own.at[i, far_at, hi], far_l.at[i], far_ss.at[1, i], far_rs.at[1, i], yl),
        )

    def now_copies(i):
        return (
            remote(own.at[i, yr_at, hi], near_l.at[i, hi], now_ss.at[0, i], now_rs.at[0, i], yr),
            remote(own.at[i, yl_at, lo], near_r.at[i, lo], now_ss.at[1, i], now_rs.at[1, i], yl),
        )

    def late_copies(i):
        return (
            remote(own.at[i, yr_at, lo], near_l.at[i, lo], late_ss.at[0, i], late_rs.at[0, i], yr),
            remote(own.at[i, yl_at, hi], near_r.at[i, hi], late_ss.at[1, i], late_rs.at[1, i], yl),
        )

    def multiply(i):
        w_copy(i).wait()
        for side, out in ((1 - core, send_a), (core, own)):
            left = attn[:, side].reshape(YN * rows, R * HD)
            part = jnp.dot(left, wbuf[i], preferred_element_type=F32)
            out[i] = part.astype(BF16).reshape(YN, rows, TILE)
        a_copy(i).start()

    def pair_sum(i):
        a_copy(i).wait_recv()
        own[i] = (own[i].astype(F32) + recv_a[i].astype(F32)).astype(BF16)
        for copy in far_copies(i) + now_copies(i):
            copy.start()

    def pass_on(i):
        to_r, to_l = far_copies(i)
        late_r, late_l = late_copies(i)
        to_r.wait_recv()
        own[i, yr_at, lo] = (own[i, yr_at, lo].astype(F32) + far_r[i].astype(F32)).astype(BF16)
        late_r.start()
        to_l.wait_recv()
        own[i, yl_at, hi] = (own[i, yl_at, hi].astype(F32) + far_l[i].astype(F32)).astype(BF16)
        late_l.start()

    row = lax.broadcasted_iota(jnp.int32, (rows, 1), 0)
    first = t * 2
    live = (row % L) < jnp.where(row < L, len_s[first], len_s[first + 1])

    def finish(i):
        for copy in now_copies(i) + late_copies(i):
            copy.wait_recv()
        at = pl.ds(pl.multiple_of(i * TILE, TILE), TILE)
        total = (
            residual[:, at].astype(F32)
            + own[i, y].astype(F32)
            + near_l[i].astype(F32)
            + near_r[i].astype(F32)
        )
        out = jnp.where(live, total, 0.0).astype(BF16)
        hidden[:, at] = out
        v = out.astype(F32)
        sq = v * v
        pr = v * head_w[:, at]
        squares[...] += functools.reduce(
            jnp.add, [sq[:, k * 128 : (k + 1) * 128] for k in range(TILE // 128)]
        )
        dots[...] += functools.reduce(
            jnp.add, [pr[:, k * 128 : (k + 1) * 128] for k in range(TILE // 128)]
        )

    def step(i, carry):
        @pl.when(i < TILES)
        def _():
            multiply(i)

        @pl.when((i >= 1) & (i < TILES + 1))
        def _():
            pair_sum(i - 1)

        @pl.when((i >= 2) & (i < TILES + 2))
        def _():
            pass_on(i - 2)

        @pl.when(i >= 3)
        def _():
            finish(i - 3)

        return carry

    lax.fori_loop(0, TILES + 3, step, 0)

    mean = jnp.sum(squares[...], axis=1, keepdims=True) * (1.0 / D)
    logit = jnp.sum(dots[...], axis=1, keepdims=True) * lax.rsqrt(mean + 1e-06)
    reward = 1.0 / (1.0 + jnp.exp(-logit))
    lane = lax.broadcasted_iota(jnp.int32, (1, 128), 1)
    wanted = jnp.full((1, 128), -1, jnp.int32)
    for k in range(8):
        wanted = jnp.where(lane == k, (k // 4) * L + mark_s[(first + k // 4) * 4 + k % 4], wanted)
    picked = jnp.where(row == wanted, reward, 0.0)
    rewards[...] = jnp.sum(picked, axis=0, keepdims=True)

    def sent(i, carry):
        a_copy(i).wait_send()
        for copy in far_copies(i) + now_copies(i) + late_copies(i):
            copy.wait_send()
        return carry

    lax.fori_loop(0, TILES, sent, 0)


def project(lens, marks, attn, weight, residual, head_w):
    dma = pltpu.SemaphoreType.DMA
    any_space = pl.BlockSpec(memory_space=pl.ANY)
    vmem = pl.BlockSpec(memory_space=pltpu.VMEM)
    smem = pl.BlockSpec(memory_space=pltpu.SMEM)
    rows = C * L // (2 * YN)
    return pl.pallas_call(
        project_kernel,
        out_shape=(
            jax.ShapeDtypeStruct((rows, D), BF16),
            jax.ShapeDtypeStruct((1, 128), F32),
        ),
        in_specs=[smem, smem, vmem, any_space, vmem, vmem],
        out_specs=(vmem, vmem),
        scratch_shapes=[
            pltpu.VMEM((TILES, R * HD, TILE), BF16),
            pltpu.VMEM((TILES, YN, rows, TILE), BF16),
            pltpu.VMEM((TILES, YN, rows, TILE), BF16),
            pltpu.VMEM((TILES, YN, rows, TILE), BF16),
            pltpu.VMEM((TILES, rows // 2, TILE), BF16),
            pltpu.VMEM((TILES, rows // 2, TILE), BF16),
            pltpu.VMEM((TILES, rows, TILE), BF16),
            pltpu.VMEM((TILES, rows, TILE), BF16),
            pltpu.VMEM((rows, 128), F32),
            pltpu.VMEM((rows, 128), F32),
            dma((TILES,)), dma((TILES,)), dma((TILES,)),
            dma((2, TILES)), dma((2, TILES)), dma((2, TILES)), dma((2, TILES)),
            dma((2, TILES)), dma((2, TILES)),
        ],
        compiler_params=pltpu.CompilerParams(
            collective_id=1, has_side_effects=True, vmem_limit_bytes=VMEM_LIMIT
        ),
        cost_estimate=pl.CostEstimate(
            flops=2 * C * L * R * HD * D, bytes_accessed=12 << 20, transcendentals=0
        ),
    )(lens, marks, attn, weight, residual, head_w)


def local(
    cand_q, cand_k, cand_v, prompt_k, prompt_v, cand_group, cand_len, boundaries,
    residual, out_weight, head_weight,
):
    attn = attend(
        cand_group, cand_q.reshape(C, L, R * HD), cand_k, cand_v, prompt_k, prompt_v
    )
    hidden, rewards = project(
        cand_len,
        boundaries.reshape(-1),
        attn.reshape(YN, 2, 2 * L, R * HD),
        out_weight,
        residual,
        head_weight.reshape(1, D),
    )
    return hidden, rewards[0, :8].reshape(2, 4)


def solution(mesh):
    in_specs = (
        P("dp", "tensor"),
        P("dp", "tensor"),
        P("dp", "tensor"),
        P("dp", "tensor"),
        P("dp", "tensor"),
        P("dp"),
        P("dp"),
        P("dp", None),
        P(("dp", "tensor"), None),
        P("tensor", None),
        P(),
    )
    out_specs = (P(("dp", "tensor"), None), P(("dp", "tensor"), None))
    return jax.shard_map(local, mesh=mesh, in_specs=in_specs, out_specs=out_specs, check_vma=False)
```

```python
import functools
import math

import jax
import jax.numpy as jnp
from jax import lax
from jax.experimental import pallas as pl
from jax.experimental.pallas import tpu as pltpu
from jax.sharding import PartitionSpec as P

HD = 128
P_SIZE = 1024
L = 32
C = 16
PAIR = 2
R = 4
XN, ZN, YN = 4, 8, 4
D = 8192
SCALE = 1.0 / math.sqrt(HD)
LOG2E = 1.4426950408889634
TILE = 512
TILES = D // 2 // TILE
ROWS = C * L // (2 * YN)
F32 = jnp.float32
BF16 = jnp.bfloat16
VMEM_LIMIT = 56 * 1024 * 1024


def remote(src, dst, send_sem, recv_sem, device):
    return pltpu.make_async_remote_copy(
        src_ref=src,
        dst_ref=dst,
        send_sem=send_sem,
        recv_sem=recv_sem,
        device_id=device,
        device_id_type=pl.DeviceIdType.MESH,
    )


def rows_of(block):
    return jnp.concatenate([block[:, r * HD : (r + 1) * HD] for r in range(R)], axis=0)


def with_ones(values):
    return jnp.concatenate([values, jnp.ones(values.shape, values.dtype)], axis=1)


def soften(scores, value_rows):
    highest = jnp.max(scores, axis=-1, keepdims=True)
    raised = jnp.exp2((scores - highest) * (SCALE * LOG2E)).astype(BF16)
    mixed = jnp.dot(raised, with_ones(value_rows), preferred_element_type=F32)
    summed = mixed[:, HD:]
    return mixed[:, :HD] / summed, highest * SCALE + jnp.log(summed)


def scores_of(queries, keys):
    return lax.dot_general(
        queries, keys, (((1,), (1,)), ((), ())), preferred_element_type=F32
    )


def fused_kernel(
    group_s, len_s, mark_s, q_in, ck_in, cv_in, pk, pv, residual_in, weight, head_in,
    hidden, rewards,
    qbuf, ck, cv, kbuf, vbuf, tabv, tabs, res, lsb, rel_r, rel_l, sfo, sfl, slot_s, scores,
    attn, attn_sib, wbuf, part, mine, far_r, far_l, near_l, near_r, residual, head_w, squares, dots,
    loc_sem, tab_ss, tab_rs, q_ss, q_rs, k_ss, k_rs, v_ss, v_rs,
    ret_ss, ret_rs, fwd_ss, fwd_rs, lse_ss, lse_rs,
    w_sem, ws_ss, ws_rs, att_ss, att_rs, far_ss, far_rs, sib_ss, sib_rs,
    now_ss, late_ss, nl_rs, nr_rs,
):
    dp = lax.axis_index("dp")
    x, z = dp // ZN, dp % ZN
    t = lax.axis_index("tensor")
    y, core = t // 2, t % 2

    def at(dp_at, t_at):
        return {"dp": dp_at, "tensor": t_at}

    xl = at(((x + XN - 1) % XN) * ZN + z, t)
    xr = at(((x + 1) % XN) * ZN + z, t)
    xx = at(((x + 2) % XN) * ZN + z, t)
    zl = at(x * ZN + (z + ZN - 1) % ZN, t)
    zr = at(x * ZN + (z + 1) % ZN, t)
    yr_at, yl_at, far_at = (y + 1) % YN, (y + YN - 1) % YN, (y + 2) % YN
    yr = [at(dp, yr_at * 2 + k) for k in range(2)]
    yl = [at(dp, yl_at * 2 + k) for k in range(2)]
    yr_same, yl_same = at(dp, yr_at * 2 + core), at(dp, yl_at * 2 + core)
    sibling = at(dp, y * 2 + 1 - core)

    barrier = pltpu.get_barrier_semaphore()
    peers = [zl, zr, xl, xr, xx, sibling] + yr + yl
    for device in peers:
        pl.semaphore_signal(
            barrier, inc=1, device_id=device, device_id_type=pl.DeviceIdType.MESH
        )

    own_k = pltpu.make_async_copy(pk, kbuf.at[0], loc_sem.at[0])
    own_v = pltpu.make_async_copy(pv, vbuf.at[0], loc_sem.at[1])
    own_q = pltpu.make_async_copy(q_in, qbuf.at[pl.ds(0, C)], loc_sem.at[2])
    own_ck = pltpu.make_async_copy(ck_in, ck, loc_sem.at[4])
    own_cv = pltpu.make_async_copy(cv_in, cv, loc_sem.at[5])
    for copy in (own_q, own_ck, own_cv, own_k, own_v):
        copy.start()

    groups = [group_s[c] for c in range(C)]
    lane = lax.broadcasted_iota(jnp.int32, (8, 128), 1)
    table = jnp.zeros((8, 128), jnp.int32)
    for c in range(C):
        slot = jnp.int32(0)
        for e in range(c):
            slot = slot + jnp.where(groups[e] == groups[c], 1, 0)
        slot = jnp.minimum(slot, PAIR - 1)
        table = jnp.where(lane == groups[c] * PAIR + slot, c, table)
        away = (groups[c] // ZN - x + XN) % XN
        region = jnp.where(away == 0, 0, jnp.where(away == 3, 4, jnp.where(away == 1, 5, 6)))
        back = (z - groups[c] % ZN + ZN) % ZN
        order = jnp.where(back == 0, 0, jnp.where(back <= 4, 2 * back - 1, 2 * (ZN - back)))
        slot_s[c] = region * C + order * PAIR + slot
    tabv[0] = table

    pl.semaphore_wait(barrier, len(peers))

    def k_to(n, src, device):
        return remote(src, kbuf.at[n], k_ss.at[n], k_rs.at[n], device)

    def v_to(n, src, device):
        return remote(src, vbuf.at[n], v_ss.at[n], v_rs.at[n], device)

    k_to(1, pk, zr).start()
    k_to(2, pk, zl).start()
    half = C // 2
    lo, hi = pl.ds(0, half), pl.ds(half, half)

    def q_copy(i, src, region, half_at, device):
        return remote(
            src, qbuf.at[pl.ds(region * C + half_at * half, half)], q_ss.at[i], q_rs.at[i], device
        )

    q_copies = [
        q_copy(0, q_in.at[lo], 1, 0, xr),
        q_copy(1, q_in.at[hi], 2, 1, xl),
        q_copy(2, q_in.at[hi], 1, 1, xr),
        q_copy(3, q_in.at[lo], 2, 0, xl),
        q_copy(4, qbuf.at[pl.ds(1 * C, half)], 3, 0, xr),
        q_copy(5, qbuf.at[pl.ds(2 * C + half, half)], 3, 1, xl),
    ]
    q_copies[0].start()
    q_copies[1].start()
    v_to(1, pv, zr).start()
    v_to(2, pv, zl).start()
    tab_copies = [
        remote(tabv.at[0], tabv.at[1], tab_ss.at[0], tab_rs.at[0], xr),
        remote(tabv.at[0], tabv.at[2], tab_ss.at[1], tab_rs.at[1], xl),
        remote(tabv.at[0], tabv.at[3], tab_ss.at[2], tab_rs.at[2], xx),
    ]
    for copy in tab_copies:
        copy.start()
    q_copies[2].start()
    q_copies[3].start()

    def w_columns(side, i):
        return weight.at[:, pl.ds(pl.multiple_of(side * (D // 2) + i * TILE, TILE), TILE)]

    def w_copy(i):
        return pltpu.make_async_copy(w_columns(core, i), wbuf.at[0, i], w_sem.at[i])

    def w_send(i):
        return remote(w_columns(1 - core, i), wbuf.at[1, i], ws_ss.at[i], ws_rs.at[i], sibling)

    def w_start(i, carry):
        w_copy(i).start()
        w_send(i).start()
        return carry

    lax.fori_loop(0, TILES, w_start, 0)
    res_copy = pltpu.make_async_copy(residual_in, residual, loc_sem.at[6])
    head_copy = pltpu.make_async_copy(head_in, head_w, loc_sem.at[7])
    res_copy.start()
    head_copy.start()

    own_q.wait()
    own_ck.wait()
    own_cv.wait()
    row = lax.broadcasted_iota(jnp.int32, (4 * R * L, 4 * L), 0)
    col = lax.broadcasted_iota(jnp.int32, (4 * R * L, 4 * L), 1)
    allowed = (row // (R * L) == col // L) & (col % L <= row % L)

    def suffix(g, carry):
        queries = jnp.concatenate([rows_of(qbuf[g * 4 + k]) for k in range(4)], axis=0)
        keys = ck[pl.ds(g * 4 * L, 4 * L), :]
        own_scores = jnp.where(allowed, scores_of(queries, keys), -1e30)
        mixed, lse = soften(own_scores, cv[pl.ds(g * 4 * L, 4 * L), :])
        for k in range(4):
            sfo[g * 4 + k] = mixed[k * R * L : (k + 1) * R * L]
            sfl[g * 4 + k] = lse[k * R * L : (k + 1) * R * L]
        return carry

    lax.fori_loop(0, C // 4, suffix, 0)

    q_copies[0].wait_recv()
    q_copies[4].start()
    q_copies[1].wait_recv()
    q_copies[5].start()
    own_k.wait()
    own_v.wait()
    for n, device in ((1, zr), (2, zl)):
        k_to(n, kbuf.at[n], device).wait_recv()
        k_to(n + 2, kbuf.at[n], device).start()
    for n, device in ((1, zr), (2, zl)):
        v_to(n, vbuf.at[n], device).wait_recv()
        v_to(n + 2, vbuf.at[n], device).start()
    for copy in tab_copies:
        copy.wait_recv()
    to_smem = pltpu.make_async_copy(tabv, tabs, loc_sem.at[3])
    to_smem.start()
    for i in (2, 3, 4, 5):
        q_copies[i].wait_recv()
    to_smem.wait()

    eye = lax.broadcasted_iota(jnp.int32, (HD, HD), 0) == lax.broadcasted_iota(
        jnp.int32, (HD, HD), 1
    )

    def pair_at(region, n):
        return pl.ds(region * C + n * PAIR, PAIR)

    def one_at(region, n, u):
        return pl.ds(region * C + n * PAIR + u, 1)

    def returns(n):
        return (
            remote(res.at[pair_at(1, n)], res.at[pair_at(5, n)], ret_ss.at[0, n], ret_rs.at[0, n], xl),
            remote(res.at[pair_at(2, n)], res.at[pair_at(4, n)], ret_ss.at[1, n], ret_rs.at[1, n], xr),
            remote(res.at[one_at(3, n, 0)], rel_r.at[pl.ds(n, 1)], ret_ss.at[2, n], ret_rs.at[2, n], xr),
            remote(res.at[one_at(3, n, 1)], rel_l.at[pl.ds(n, 1)], ret_ss.at[3, n], ret_rs.at[3, n], xl),
        )

    def relays(n):
        return (
            remote(rel_r.at[pl.ds(n, 1)], res.at[one_at(6, n, 0)], fwd_ss.at[0, n], fwd_rs.at[0, n], xr),
            remote(rel_l.at[pl.ds(n, 1)], res.at[one_at(6, n, 1)], fwd_ss.at[1, n], fwd_rs.at[1, n], xl),
        )

    def relay(n):
        _, _, right, left = returns(n)
        on_right, on_left = relays(n)
        right.wait_recv()
        on_right.start()
        left.wait_recv()
        on_left.start()

    def step(n, carry):
        @pl.when(n == 2)
        def _():
            for m, device in ((3, zr), (4, zl)):
                k_to(m, kbuf.at[m], device).wait_recv()
                k_to(m + 2, kbuf.at[m], device).start()

        @pl.when(n == 3)
        def _():
            for m, device in ((3, zr), (4, zl)):
                v_to(m, vbuf.at[m], device).wait_recv()
                v_to(m + 2, vbuf.at[m], device).start()

        @pl.when(n == 5)
        def _():
            k_to(5, kbuf.at[5], zr).wait_recv()
            k_to(7, kbuf.at[5], zr).start()
            k_to(6, kbuf.at[6], zl).wait_recv()
            v_to(6, vbuf.at[6], zl).wait_recv()
            v_to(7, vbuf.at[6], zl).start()
            v_to(5, vbuf.at[5], zr).wait_recv()

        @pl.when(n == 7)
        def _():
            k_to(7, kbuf.at[5], zr).wait_recv()
            v_to(7, vbuf.at[6], zl).wait_recv()

        owner_z = (z + (1 - 2 * (n % 2)) * ((n + 1) // 2) + ZN) % ZN
        base = (x * ZN + owner_z) * PAIR

        def queries_of(s):
            return jnp.concatenate(
                [rows_of(qbuf[s * C + tabs[s, 0, base + u]]) for u in range(PAIR)], axis=0
            )

        scores[0] = scores_of(queries_of(0), kbuf[n])
        for s in range(XN):
            if s + 1 < XN:
                scores[(s + 1) % 2] = scores_of(queries_of(s + 1), kbuf[n])
            mixed, lse = soften(scores[s % 2], vbuf[n])
            mixed = mixed.astype(BF16)
            for u in range(PAIR):
                here = s * C + n * PAIR + u
                for r in range(R):
                    first = (u * R + r) * L
                    res[here, :, r * HD : (r + 1) * HD] = mixed[first : first + L]
                lsb[here] = jnp.sum(
                    jnp.where(eye, lse[u * HD : (u + 1) * HD], 0.0), axis=0, keepdims=True
                )
        for copy in returns(n):
            copy.start()

        @pl.when(n >= 2)
        def _():
            relay(n - 2)

        return carry

    lax.fori_loop(0, ZN, step, 0)
    lse_copies = [
        remote(lsb.at[pl.ds(1 * C, C)], lsb.at[pl.ds(5 * C, C)], lse_ss.at[0], lse_rs.at[0], xl),
        remote(lsb.at[pl.ds(2 * C, C)], lsb.at[pl.ds(4 * C, C)], lse_ss.at[1], lse_rs.at[1], xr),
        remote(lsb.at[pl.ds(3 * C, C)], lsb.at[pl.ds(6 * C, C)], lse_ss.at[2], lse_rs.at[2], xx),
    ]
    for copy in lse_copies:
        copy.start()
    relay(ZN - 2)
    relay(ZN - 1)

    def arrived(n, carry):
        from_xl, from_xr, _, _ = returns(n)
        from_xl.wait_recv()
        from_xr.wait_recv()
        for copy in relays(n):
            copy.wait_recv()
        return carry

    lax.fori_loop(0, ZN, arrived, 0)
    for copy in lse_copies:
        copy.wait_recv()

    def attn_copy(g):
        quarter = pl.ds(g * 4, 4)
        return remote(attn.at[quarter], attn_sib.at[quarter], att_ss.at[g], att_rs.at[g], sibling)

    def merge(g, carry):
        for k in range(4):
            c = g * 4 + k
            where = slot_s[c]
            prefix = rows_of(res[where]).astype(F32)
            prefix_lse = jnp.sum(jnp.where(eye, lsb[where], 0.0), axis=1, keepdims=True)
            suffix_lse = sfl[c]
            largest = jnp.maximum(prefix_lse, suffix_lse)
            a = jnp.exp(prefix_lse - largest)
            b = jnp.exp(suffix_lse - largest)
            joined = ((a * prefix + b * sfo[c]) / (a + b)).astype(BF16)
            for r in range(R):
                attn[c, :, r * HD : (r + 1) * HD] = joined[r * L : (r + 1) * L]
        attn_copy(g).start()
        return carry

    lax.fori_loop(0, C // 4, merge, 0)

    squares[...] = jnp.zeros_like(squares)
    dots[...] = jnp.zeros_like(dots)

    def far_copies(i):
        return (
            remote(part.at[i, far_at, 0], far_r.at[i], far_ss.at[0, i], far_rs.at[0, i], yr_same),
            remote(part.at[i, far_at, 1], far_l.at[i], far_ss.at[1, i], far_rs.at[1, i], yl_same),
        )

    def now_copies(i):
        return (
            remote(part.at[i, yr_at, 1], near_l.at[core, i], now_ss.at[0, i], nl_rs.at[core, i], yr[1]),
            remote(part.at[i, yl_at, 0], near_r.at[core, i], now_ss.at[1, i], nr_rs.at[core, i], yl[0]),
        )

    def late_copies(i):
        return (
            remote(part.at[i, yr_at, 0], near_l.at[core, i], late_ss.at[0, i], nl_rs.at[core, i], yr[0]),
            remote(part.at[i, yl_at, 1], near_r.at[core, i], late_ss.at[1, i], nr_rs.at[core, i], yl[1]),
        )

    def sib_copy(i):
        return remote(part.at[i, y, 1 - core], mine.at[i], sib_ss.at[i], sib_rs.at[i], sibling)

    def near_copies(i, side):
        return (
            remote(near_l.at[side, i], near_l.at[side, i], now_ss.at[0, i], nl_rs.at[side, i], yr[1]),
            remote(near_r.at[side, i], near_r.at[side, i], now_ss.at[1, i], nr_rs.at[side, i], yl[0]),
        )

    def multiply(i):
        w_copy(i).wait()
        w_send(i).wait_recv()
        summed = jnp.dot(
            attn[...].reshape(C * L, R * HD), wbuf[0, i], preferred_element_type=F32
        ) + jnp.dot(
            attn_sib[...].reshape(C * L, R * HD), wbuf[1, i], preferred_element_type=F32
        )
        part[i] = summed.astype(BF16).reshape(YN, 2, ROWS, TILE)
        for copy in far_copies(i) + now_copies(i) + (sib_copy(i),):
            copy.start()

    def pass_on(i):
        to_r, to_l = far_copies(i)
        late_r, late_l = late_copies(i)
        to_r.wait_recv()
        part[i, yr_at, 0] = (part[i, yr_at, 0].astype(F32) + far_r[i].astype(F32)).astype(BF16)
        late_r.start()
        to_l.wait_recv()
        part[i, yl_at, 1] = (part[i, yl_at, 1].astype(F32) + far_l[i].astype(F32)).astype(BF16)
        late_l.start()

    token = lax.broadcasted_iota(jnp.int32, (ROWS, 1), 0)
    first_cand = t * 2
    live = (token % L) < jnp.where(token < L, len_s[first_cand], len_s[first_cand + 1])

    def finish(i):
        sib_copy(i).wait_recv()
        for side in range(2):
            for copy in near_copies(i, side):
                copy.wait_recv()
        for side, kept in ((core, part[i, y, core]), (1 - core, mine[i])):
            columns = pl.ds(pl.multiple_of(side * (D // 2) + i * TILE, TILE), TILE)
            total = (
                residual[:, columns].astype(F32)
                + kept.astype(F32)
                + near_l[side, i].astype(F32)
                + near_r[side, i].astype(F32)
            )
            out = jnp.where(live, total, 0.0).astype(BF16)
            hidden[:, columns] = out
            v = out.astype(F32)
            sq = v * v
            pr = v * head_w[:, columns]
            squares[...] += functools.reduce(
                jnp.add, [sq[:, k * 128 : (k + 1) * 128] for k in range(TILE // 128)]
            )
            dots[...] += functools.reduce(
                jnp.add, [pr[:, k * 128 : (k + 1) * 128] for k in range(TILE // 128)]
            )

    for g in range(C // 4):
        attn_copy(g).wait_recv()
    res_copy.wait()
    head_copy.wait()

    def tile_step(i, carry):
        @pl.when(i < TILES)
        def _():
            multiply(i)

        @pl.when((i >= 1) & (i < TILES + 1))
        def _():
            pass_on(i - 1)

        @pl.when(i >= 2)
        def _():
            finish(i - 2)

        return carry

    lax.fori_loop(0, TILES + 2, tile_step, 0)

    mean = jnp.sum(squares[...], axis=1, keepdims=True) * (1.0 / D)
    logit = jnp.sum(dots[...], axis=1, keepdims=True) * lax.rsqrt(mean + 1e-06)
    reward = 1.0 / (1.0 + jnp.exp(-logit))
    lane_row = lax.broadcasted_iota(jnp.int32, (1, 128), 1)
    for a in range(2):
        wanted = jnp.full((1, 128), -1, jnp.int32)
        for k in range(4):
            wanted = jnp.where(lane_row == k, a * L + mark_s[k, first_cand + a], wanted)
        picked = jnp.sum(jnp.where(token == wanted, reward, 0.0), axis=0, keepdims=True)
        rewards[a : a + 1, :] = picked[:, :4]

    def sent(n, carry):
        for copy in returns(n) + relays(n):
            copy.wait_send()
        return carry

    lax.fori_loop(0, ZN, sent, 0)
    for copy in lse_copies + q_copies + tab_copies:
        copy.wait_send()
    for n in range(1, ZN):
        k_to(n, kbuf.at[0], zr).wait_send()
        v_to(n, vbuf.at[0], zr).wait_send()
    for g in range(C // 4):
        attn_copy(g).wait_send()

    def tile_sent(i, carry):
        w_send(i).wait_send()
        sib_copy(i).wait_send()
        for copy in far_copies(i) + now_copies(i) + late_copies(i):
            copy.wait_send()
        return carry

    lax.fori_loop(0, TILES, tile_sent, 0)


def fused(group, lens, marks, q, ck, cv, pk, pv, residual, weight, head_w):
    dma = pltpu.SemaphoreType.DMA
    any_space = pl.BlockSpec(memory_space=pl.ANY)
    vmem = pl.BlockSpec(memory_space=pltpu.VMEM)
    smem = pl.BlockSpec(memory_space=pltpu.SMEM)
    return pl.pallas_call(
        fused_kernel,
        out_shape=(
            jax.ShapeDtypeStruct((ROWS, D), BF16),
            jax.ShapeDtypeStruct((2, 4), F32),
        ),
        in_specs=[smem] * 3 + [any_space] * 8,
        out_specs=(vmem, vmem),
        scratch_shapes=[
            pltpu.VMEM((XN * C, L, R * HD), BF16),
            pltpu.VMEM((C * L, HD), BF16),
            pltpu.VMEM((C * L, HD), BF16),
            pltpu.VMEM((ZN, P_SIZE, HD), BF16),
            pltpu.VMEM((ZN, P_SIZE, HD), BF16),
            pltpu.VMEM((XN, 8, 128), jnp.int32),
            pltpu.SMEM((XN, 8, 128), jnp.int32),
            pltpu.VMEM((7 * C, L, R * HD), BF16),
            pltpu.VMEM((7 * C, 1, HD), F32),
            pltpu.VMEM((ZN, L, R * HD), BF16),
            pltpu.VMEM((ZN, L, R * HD), BF16),
            pltpu.VMEM((C, R * L, HD), F32),
            pltpu.VMEM((C, R * L, HD), F32),
            pltpu.SMEM((C,), jnp.int32),
            pltpu.VMEM((2, PAIR * R * L, P_SIZE), F32),
            pltpu.VMEM((C, L, R * HD), BF16),
            pltpu.VMEM((C, L, R * HD), BF16),
            pltpu.VMEM((2, TILES, R * HD, TILE), BF16),
            pltpu.VMEM((TILES, YN, 2, ROWS, TILE), BF16),
            pltpu.VMEM((TILES, ROWS, TILE), BF16),
            pltpu.VMEM((TILES, ROWS, TILE), BF16),
            pltpu.VMEM((TILES, ROWS, TILE), BF16),
            pltpu.VMEM((2, TILES, ROWS, TILE), BF16),
            pltpu.VMEM((2, TILES, ROWS, TILE), BF16),
            pltpu.VMEM((ROWS, D), BF16),
            pltpu.VMEM((1, D), F32),
            pltpu.VMEM((ROWS, 128), F32),
            pltpu.VMEM((ROWS, 128), F32),
            dma((8,)), dma((3,)), dma((3,)), dma((6,)), dma((6,)),
            dma((ZN,)), dma((ZN,)), dma((ZN,)), dma((ZN,)),
            dma((4, ZN)), dma((4, ZN)), dma((2, ZN)), dma((2, ZN)), dma((3,)), dma((3,)),
            dma((TILES,)), dma((TILES,)), dma((TILES,)), dma((4,)), dma((4,)),
            dma((2, TILES)), dma((2, TILES)), dma((TILES,)), dma((TILES,)),
            dma((2, TILES)), dma((2, TILES)), dma((2, TILES)), dma((2, TILES)),
        ],
        compiler_params=pltpu.CompilerParams(
            collective_id=0, has_side_effects=True, vmem_limit_bytes=VMEM_LIMIT
        ),
        cost_estimate=pl.CostEstimate(
            flops=2 * 2 * 64 * 128 * P_SIZE * HD + 2 * C * L * R * HD * D,
            bytes_accessed=16 << 20,
            transcendentals=8 << 20,
        ),
    )(group, lens, marks, q, ck, cv, pk, pv, residual, weight, head_w)


def local(
    cand_q, cand_k, cand_v, prompt_k, prompt_v, cand_group, cand_len, boundaries,
    residual, out_weight, head_weight,
):
    hidden, rewards = fused(
        cand_group,
        cand_len,
        boundaries.T,
        cand_q.reshape(C, L, R * HD),
        cand_k,
        cand_v,
        prompt_k,
        prompt_v,
        residual,
        out_weight,
        head_weight.reshape(1, D),
    )
    return hidden, rewards


def solution(mesh):
    in_specs = (
        P("dp", "tensor"),
        P("dp", "tensor"),
        P("dp", "tensor"),
        P("dp", "tensor"),
        P("dp", "tensor"),
        P("dp"),
        P("dp"),
        P("dp", None),
        P(("dp", "tensor"), None),
        P("tensor", None),
        P(),
    )
    out_specs = (P(("dp", "tensor"), None), P(("dp", "tensor"), None))
    return jax.shard_map(local, mesh=mesh, in_specs=in_specs, out_specs=out_specs, check_vma=False)
```

```python
import functools
import math

import jax
import jax.numpy as jnp
from jax import lax
from jax.experimental import pallas as pl
from jax.experimental.pallas import tpu as pltpu
from jax.sharding import PartitionSpec as P

HD = 128
P_SIZE = 1024
L = 32
C = 16
PAIR = 2
R = 4
XN, ZN, YN = 4, 8, 4
D = 8192
SCALE = 1.0 / math.sqrt(HD)
LOG2E = 1.4426950408889634
TILE = 512
TILES = D // 2 // TILE
AHEAD, BEHIND = 2, 4
ROWS = C * L // (2 * YN)
F32 = jnp.float32
BF16 = jnp.bfloat16
VMEM_LIMIT = 56 * 1024 * 1024


def remote(src, dst, send_sem, recv_sem, device):
    return pltpu.make_async_remote_copy(
        src_ref=src,
        dst_ref=dst,
        send_sem=send_sem,
        recv_sem=recv_sem,
        device_id=device,
        device_id_type=pl.DeviceIdType.MESH,
    )


def rows_of(block):
    return jnp.concatenate([block[:, r * HD : (r + 1) * HD] for r in range(R)], axis=0)


def with_ones(values):
    return jnp.concatenate([values, jnp.ones(values.shape, values.dtype)], axis=1)


def soften(scores, value_rows):
    highest = jnp.max(scores, axis=-1, keepdims=True)
    raised = jnp.exp2((scores - highest) * (SCALE * LOG2E)).astype(BF16)
    mixed = jnp.dot(raised, with_ones(value_rows), preferred_element_type=F32)
    summed = mixed[:, HD:]
    return mixed[:, :HD] / summed, highest * SCALE + jnp.log(summed)


def scores_of(queries, keys):
    return lax.dot_general(
        queries, keys, (((1,), (1,)), ((), ())), preferred_element_type=F32
    )


def fused_kernel(
    group_s, len_s, mark_s, q_in, ck_in, cv_in, pk, pv, residual_in, weight, head_in,
    hidden, rewards,
    qbuf, ck, cv, kbuf, vbuf, tabv, tabs, res, lsb, rel_r, rel_l, sfo, sfl, slot_s, scores,
    attn, attn_sib, wbuf, part, far, near, residual, head_w, squares, dots,
    loc_sem, tab_ss, tab_rs, q_ss, q_rs, k_ss, k_rs, v_ss, v_rs,
    ret_ss, ret_rs, rel_rs, fwd_ss, lse_ss, lse_rs,
    w_sem, ws_ss, ws_rs, att_ss, att_rs, far_ss, far_rs, sib_ss, now_ss, late_ss, near_rs,
):
    dp = lax.axis_index("dp")
    x, z = dp // ZN, dp % ZN
    t = lax.axis_index("tensor")
    y, core = t // 2, t % 2

    def at(dp_at, t_at):
        return {"dp": dp_at, "tensor": t_at}

    xl = at(((x + XN - 1) % XN) * ZN + z, t)
    xr = at(((x + 1) % XN) * ZN + z, t)
    xx = at(((x + 2) % XN) * ZN + z, t)
    zl = at(x * ZN + (z + ZN - 1) % ZN, t)
    zr = at(x * ZN + (z + 1) % ZN, t)
    yr_at, yl_at, far_at = (y + 1) % YN, (y + YN - 1) % YN, (y + 2) % YN
    yr = [at(dp, yr_at * 2 + k) for k in range(2)]
    yl = [at(dp, yl_at * 2 + k) for k in range(2)]
    yr_same, yl_same = at(dp, yr_at * 2 + core), at(dp, yl_at * 2 + core)
    sibling = at(dp, y * 2 + 1 - core)

    barrier = pltpu.get_barrier_semaphore()
    peers = [zl, zr, xl, xr, xx, sibling] + yr + yl
    for device in peers:
        pl.semaphore_signal(
            barrier, inc=1, device_id=device, device_id_type=pl.DeviceIdType.MESH
        )

    pl.semaphore_wait(barrier, len(peers))

    def k_to(n, src, device):
        return remote(src, kbuf.at[n], k_ss, k_rs.at[n], device)

    def v_to(n, src, device):
        return remote(src, vbuf.at[n], v_ss, v_rs.at[n], device)

    k_to(1, pk, zr).start()
    k_to(2, pk, zl).start()
    half = C // 2
    lo, hi = pl.ds(0, half), pl.ds(half, half)

    def q_copy(i, src, region, half_at, device):
        return remote(
            src, qbuf.at[pl.ds(region * C + half_at * half, half)], q_ss, q_rs.at[min(i, 2)], device
        )

    q_copies = [
        q_copy(0, q_in.at[lo], 1, 0, xr),
        q_copy(1, q_in.at[hi], 2, 1, xl),
        q_copy(2, q_in.at[hi], 1, 1, xr),
        q_copy(3, q_in.at[lo], 2, 0, xl),
        q_copy(4, qbuf.at[pl.ds(1 * C, half)], 3, 0, xr),
        q_copy(5, qbuf.at[pl.ds(2 * C + half, half)], 3, 1, xl),
    ]
    q_copies[0].start()
    q_copies[1].start()
    v_to(1, pv, zr).start()
    v_to(2, pv, zl).start()
    q_copies[2].start()
    q_copies[3].start()
    own_k = pltpu.make_async_copy(pk, kbuf.at[0], loc_sem.at[0])
    own_v = pltpu.make_async_copy(pv, vbuf.at[0], loc_sem.at[1])
    own_q = pltpu.make_async_copy(q_in, qbuf.at[pl.ds(0, C)], loc_sem.at[2])
    own_ck = pltpu.make_async_copy(ck_in, ck, loc_sem.at[4])
    own_cv = pltpu.make_async_copy(cv_in, cv, loc_sem.at[5])
    for copy in (own_q, own_ck, own_cv, own_k, own_v):
        copy.start()
    groups = [group_s[c] for c in range(C)]
    lane = lax.broadcasted_iota(jnp.int32, (8, 128), 1)
    table = jnp.zeros((8, 128), jnp.int32)
    for c in range(C):
        slot = jnp.int32(0)
        for e in range(c):
            slot = slot + jnp.where(groups[e] == groups[c], 1, 0)
        slot = jnp.minimum(slot, PAIR - 1)
        table = jnp.where(lane == groups[c] * PAIR + slot, c, table)
        away = (groups[c] // ZN - x + XN) % XN
        region = jnp.where(away == 0, 0, jnp.where(away == 3, 4, jnp.where(away == 1, 5, 6)))
        back = (z - groups[c] % ZN + ZN) % ZN
        order = jnp.where(back == 0, 0, jnp.where(back <= 4, 2 * back - 1, 2 * (ZN - back)))
        slot_s[c] = region * C + order * PAIR + slot
    tabv[0] = table
    tab_copies = [
        remote(tabv.at[0], tabv.at[1], tab_ss, tab_rs, xr),
        remote(tabv.at[0], tabv.at[2], tab_ss, tab_rs, xl),
        remote(tabv.at[0], tabv.at[3], tab_ss, tab_rs, xx),
    ]
    for copy in tab_copies:
        copy.start()

    def w_columns(side, i):
        return weight.at[:, pl.ds(pl.multiple_of(side * (D // 2) + i * TILE, TILE), TILE)]

    def w_copy(i):
        return pltpu.make_async_copy(w_columns(core, i), wbuf.at[0, i], w_sem)

    def w_send(i):
        return remote(w_columns(1 - core, i), wbuf.at[1, i], ws_ss, ws_rs, sibling)

    def w_start(i, carry):
        w_copy(i).start()
        w_send(i).start()
        return carry

    lax.fori_loop(0, TILES, w_start, 0)
    res_copy = pltpu.make_async_copy(residual_in, residual, loc_sem.at[6])
    head_copy = pltpu.make_async_copy(head_in, head_w, loc_sem.at[7])
    res_copy.start()
    head_copy.start()

    own_q.wait()
    own_ck.wait()
    own_cv.wait()
    row = lax.broadcasted_iota(jnp.int32, (4 * R * L, 4 * L), 0)
    col = lax.broadcasted_iota(jnp.int32, (4 * R * L, 4 * L), 1)
    allowed = (row // (R * L) == col // L) & (col % L <= row % L)

    def suffix(g, carry):
        queries = jnp.concatenate([rows_of(qbuf[g * 4 + k]) for k in range(4)], axis=0)
        keys = ck[pl.ds(g * 4 * L, 4 * L), :]
        own_scores = jnp.where(allowed, scores_of(queries, keys), -1e30)
        mixed, lse = soften(own_scores, cv[pl.ds(g * 4 * L, 4 * L), :])
        for k in range(4):
            sfo[g * 4 + k] = mixed[k * R * L : (k + 1) * R * L]
            sfl[g * 4 + k] = lse[k * R * L : (k + 1) * R * L]
        return carry

    lax.fori_loop(0, C // 4, suffix, 0)

    q_copies[0].wait_recv()
    q_copies[4].start()
    q_copies[1].wait_recv()
    q_copies[5].start()
    own_k.wait()
    own_v.wait()
    for n, device in ((1, zr), (2, zl)):
        k_to(n, kbuf.at[n], device).wait_recv()
        k_to(n + 2, kbuf.at[n], device).start()
    for n, device in ((1, zr), (2, zl)):
        v_to(n, vbuf.at[n], device).wait_recv()
        v_to(n + 2, vbuf.at[n], device).start()
    tab_all = remote(tabv.at[pl.ds(1, 3)], tabv.at[pl.ds(1, 3)], tab_ss, tab_rs, xl)
    tab_all.wait_recv()
    to_smem = pltpu.make_async_copy(tabv, tabs, loc_sem.at[3])
    to_smem.start()
    q_rest = qbuf.at[pl.ds(2 * C, 2 * C)]
    remote(q_rest, q_rest, q_ss, q_rs.at[2], xl).wait_recv()
    to_smem.wait()

    eye = lax.broadcasted_iota(jnp.int32, (HD, HD), 0) == lax.broadcasted_iota(
        jnp.int32, (HD, HD), 1
    )

    def pair_at(region, n):
        return pl.ds(region * C + n * PAIR, PAIR)

    def one_at(region, n, u):
        return pl.ds(region * C + n * PAIR + u, 1)

    def returns(n):
        return (
            remote(res.at[pair_at(1, n)], res.at[pair_at(5, n)], ret_ss, ret_rs, xl),
            remote(res.at[pair_at(2, n)], res.at[pair_at(4, n)], ret_ss, ret_rs, xr),
            remote(res.at[one_at(3, n, 0)], rel_r.at[pl.ds(n, 1)], ret_ss, rel_rs.at[0, n], xr),
            remote(res.at[one_at(3, n, 1)], rel_l.at[pl.ds(n, 1)], ret_ss, rel_rs.at[1, n], xl),
        )

    def relays(n):
        return (
            remote(rel_r.at[pl.ds(n, 1)], res.at[one_at(6, n, 0)], fwd_ss, ret_rs, xr),
            remote(rel_l.at[pl.ds(n, 1)], res.at[one_at(6, n, 1)], fwd_ss, ret_rs, xl),
        )

    def relay(n):
        _, _, right, left = returns(n)
        on_right, on_left = relays(n)
        right.wait_recv()
        on_right.start()
        left.wait_recv()
        on_left.start()

    def step(n, carry):
        @pl.when(n == 2)
        def _():
            for m, device in ((3, zr), (4, zl)):
                k_to(m, kbuf.at[m], device).wait_recv()
                k_to(m + 2, kbuf.at[m], device).start()

        @pl.when(n == 3)
        def _():
            for m, device in ((3, zr), (4, zl)):
                v_to(m, vbuf.at[m], device).wait_recv()
                v_to(m + 2, vbuf.at[m], device).start()

        @pl.when(n == 5)
        def _():
            k_to(5, kbuf.at[5], zr).wait_recv()
            k_to(7, kbuf.at[5], zr).start()
            k_to(6, kbuf.at[6], zl).wait_recv()
            v_to(6, vbuf.at[6], zl).wait_recv()
            v_to(7, vbuf.at[6], zl).start()
            v_to(5, vbuf.at[5], zr).wait_recv()

        @pl.when(n == 7)
        def _():
            k_to(7, kbuf.at[5], zr).wait_recv()
            v_to(7, vbuf.at[6], zl).wait_recv()

        owner_z = (z + (1 - 2 * (n % 2)) * ((n + 1) // 2) + ZN) % ZN
        base = (x * ZN + owner_z) * PAIR

        def queries_of(s):
            return jnp.concatenate(
                [rows_of(qbuf[s * C + tabs[s, 0, base + u]]) for u in range(PAIR)], axis=0
            )

        scores[0] = scores_of(queries_of(0), kbuf[n])
        for s in range(XN):
            if s + 1 < XN:
                scores[(s + 1) % 2] = scores_of(queries_of(s + 1), kbuf[n])
            mixed, lse = soften(scores[s % 2], vbuf[n])
            mixed = mixed.astype(BF16)
            for u in range(PAIR):
                here = s * C + n * PAIR + u
                for r in range(R):
                    first = (u * R + r) * L
                    res[here, :, r * HD : (r + 1) * HD] = mixed[first : first + L]
                lsb[here] = jnp.sum(
                    jnp.where(eye, lse[u * HD : (u + 1) * HD], 0.0), axis=0, keepdims=True
                )
        for copy in returns(n):
            copy.start()

        @pl.when(n >= 2)
        def _():
            relay(n - 2)

        return carry

    lax.fori_loop(0, ZN, step, 0)
    lse_copies = [
        remote(lsb.at[pl.ds(1 * C, C)], lsb.at[pl.ds(5 * C, C)], lse_ss, lse_rs, xl),
        remote(lsb.at[pl.ds(2 * C, C)], lsb.at[pl.ds(4 * C, C)], lse_ss, lse_rs, xr),
        remote(lsb.at[pl.ds(3 * C, C)], lsb.at[pl.ds(6 * C, C)], lse_ss, lse_rs, xx),
    ]
    for copy in lse_copies:
        copy.start()
    relay(ZN - 2)
    relay(ZN - 1)

    came = pl.ds(4 * C, 3 * C)
    res_all = remote(res.at[came], res.at[came], fwd_ss, ret_rs, xl)
    lse_all = remote(lsb.at[came], lsb.at[came], lse_ss, lse_rs, xl)
    res_all.wait_recv()
    lse_all.wait_recv()

    def attn_copy(g):
        quarter = pl.ds(g * 4, 4)
        return remote(attn.at[quarter], attn_sib.at[quarter], att_ss, att_rs, sibling)

    def merge(g, carry):
        for k in range(4):
            c = g * 4 + k
            where = slot_s[c]
            prefix = rows_of(res[where]).astype(F32)
            prefix_lse = jnp.sum(jnp.where(eye, lsb[where], 0.0), axis=1, keepdims=True)
            suffix_lse = sfl[c]
            largest = jnp.maximum(prefix_lse, suffix_lse)
            a = jnp.exp(prefix_lse - largest)
            b = jnp.exp(suffix_lse - largest)
            joined = ((a * prefix + b * sfo[c]) / (a + b)).astype(BF16)
            for r in range(R):
                attn[c, :, r * HD : (r + 1) * HD] = joined[r * L : (r + 1) * L]
        attn_copy(g).start()
        return carry

    lax.fori_loop(0, C // 4, merge, 0)

    squares[...] = jnp.zeros_like(squares)
    dots[...] = jnp.zeros_like(dots)

    def far_copies(i):
        return (
            remote(part.at[i, far_at, 0], far.at[i, 0], far_ss, far_rs.at[i], yr_same),
            remote(part.at[i, far_at, 1], far.at[i, 1], far_ss, far_rs.at[i], yl_same),
        )

    def now_copies(i):
        return (
            remote(part.at[i, yr_at, 1], near.at[i, core], now_ss, near_rs.at[i], yr[1]),
            remote(part.at[i, yl_at, 0], near.at[i, 2 + core], now_ss, near_rs.at[i], yl[0]),
        )

    def late_copies(i):
        return (
            remote(part.at[i, yr_at, 0], near.at[i, core], late_ss, near_rs.at[i], yr[0]),
            remote(part.at[i, yl_at, 1], near.at[i, 2 + core], late_ss, near_rs.at[i], yl[1]),
        )

    def sib_copy(i):
        return remote(part.at[i, y, 1 - core], near.at[i, 4], sib_ss, near_rs.at[i], sibling)

    def multiply(i):
        summed = jnp.dot(
            attn[...].reshape(C * L, R * HD), wbuf[0, i], preferred_element_type=F32
        ) + jnp.dot(
            attn_sib[...].reshape(C * L, R * HD), wbuf[1, i], preferred_element_type=F32
        )
        part[i] = summed.astype(BF16).reshape(YN, 2, ROWS, TILE)
        for copy in far_copies(i) + now_copies(i) + (sib_copy(i),):
            copy.start()

    def pass_on(i):
        late_r, late_l = late_copies(i)
        remote(far.at[i], far.at[i], far_ss, far_rs.at[i], yr_same).wait_recv()
        part[i, yr_at, 0] = (part[i, yr_at, 0].astype(F32) + far[i, 0].astype(F32)).astype(BF16)
        late_r.start()
        part[i, yl_at, 1] = (part[i, yl_at, 1].astype(F32) + far[i, 1].astype(F32)).astype(BF16)
        late_l.start()

    token = lax.broadcasted_iota(jnp.int32, (ROWS, 1), 0)
    first_cand = t * 2
    live = (token % L) < jnp.where(token < L, len_s[first_cand], len_s[first_cand + 1])

    def finish(i):
        remote(near.at[i], near.at[i], now_ss, near_rs.at[i], yr_same).wait_recv()
        for side, kept in ((core, part[i, y, core]), (1 - core, near[i, 4])):
            columns = pl.ds(pl.multiple_of(side * (D // 2) + i * TILE, TILE), TILE)
            total = (
                residual[:, columns].astype(F32)
                + kept.astype(F32)
                + near[i, side].astype(F32)
                + near[i, 2 + side].astype(F32)
            )
            out = jnp.where(live, total, 0.0).astype(BF16)
            hidden[:, columns] = out
            v = out.astype(F32)
            sq = v * v
            pr = v * head_w[:, columns]
            squares[...] += functools.reduce(
                jnp.add, [sq[:, k * 128 : (k + 1) * 128] for k in range(TILE // 128)]
            )
            dots[...] += functools.reduce(
                jnp.add, [pr[:, k * 128 : (k + 1) * 128] for k in range(TILE // 128)]
            )

    pltpu.make_async_copy(wbuf.at[0], wbuf.at[0], w_sem).wait()
    w_all = remote(wbuf.at[1], wbuf.at[1], ws_ss, ws_rs, sibling)
    w_all.wait_recv()
    attn_all = remote(attn, attn_sib, att_ss, att_rs, sibling)
    attn_all.wait_recv()
    res_copy.wait()
    head_copy.wait()

    def all_sent():
        others, queries = pl.ds(1, ZN - 1), pl.ds(C, 3 * C)
        for copy in (
            remote(kbuf.at[others], kbuf.at[others], k_ss, k_rs.at[0], zr),
            remote(vbuf.at[others], vbuf.at[others], v_ss, v_rs.at[0], zr),
            remote(qbuf.at[queries], qbuf.at[queries], q_ss, q_rs.at[0], xr),
            remote(res.at[queries], res.at[queries], ret_ss, ret_rs, xr),
            remote(res.at[pl.ds(0, C)], res.at[pl.ds(0, C)], fwd_ss, ret_rs, xr),
            tab_all, lse_all, w_all, attn_all,
        ):
            copy.wait_send()

    def tile_step(i, carry):
        @pl.when(i < TILES)
        def _():
            multiply(i)

        @pl.when((i >= AHEAD) & (i < TILES + AHEAD))
        def _():
            pass_on(i - AHEAD)

        @pl.when(i >= BEHIND)
        def _():
            finish(i - BEHIND)

        return carry

    lax.fori_loop(0, TILES + BEHIND, tile_step, 0)
    all_sent()
    tiles = near.at[:, pl.ds(0, 2)]
    for sem in (far_ss, now_ss, late_ss):
        remote(tiles, tiles, sem, near_rs.at[0], yr_same).wait_send()
    remote(far.at[:, 0], far.at[:, 0], sib_ss, near_rs.at[0], sibling).wait_send()

    mean = jnp.sum(squares[...], axis=1, keepdims=True) * (1.0 / D)
    logit = jnp.sum(dots[...], axis=1, keepdims=True) * lax.rsqrt(mean + 1e-06)
    reward = 1.0 / (1.0 + jnp.exp(-logit))
    lane_row = lax.broadcasted_iota(jnp.int32, (1, 128), 1)
    for a in range(2):
        wanted = jnp.full((1, 128), -1, jnp.int32)
        for k in range(4):
            wanted = jnp.where(lane_row == k, a * L + mark_s[k, first_cand + a], wanted)
        picked = jnp.sum(jnp.where(token == wanted, reward, 0.0), axis=0, keepdims=True)
        rewards[a : a + 1, :] = picked[:, :4]


def fused(group, lens, marks, q, ck, cv, pk, pv, residual, weight, head_w):
    dma = pltpu.SemaphoreType.DMA
    any_space = pl.BlockSpec(memory_space=pl.ANY)
    vmem = pl.BlockSpec(memory_space=pltpu.VMEM)
    smem = pl.BlockSpec(memory_space=pltpu.SMEM)
    return pl.pallas_call(
        fused_kernel,
        out_shape=(
            pltpu.VMEM((ROWS, D), BF16),
            pltpu.VMEM((2, 4), F32),
        ),
        in_specs=[smem] * 3 + [any_space] * 8,
        out_specs=(vmem, vmem),
        scratch_shapes=[
            pltpu.VMEM((XN * C, L, R * HD), BF16),
            pltpu.VMEM((C * L, HD), BF16),
            pltpu.VMEM((C * L, HD), BF16),
            pltpu.VMEM((ZN, P_SIZE, HD), BF16),
            pltpu.VMEM((ZN, P_SIZE, HD), BF16),
            pltpu.VMEM((XN, 8, 128), jnp.int32),
            pltpu.SMEM((XN, 8, 128), jnp.int32),
            pltpu.VMEM((7 * C, L, R * HD), BF16),
            pltpu.VMEM((7 * C, 1, HD), F32),
            pltpu.VMEM((ZN, L, R * HD), BF16),
            pltpu.VMEM((ZN, L, R * HD), BF16),
            pltpu.VMEM((C, R * L, HD), F32),
            pltpu.VMEM((C, R * L, HD), F32),
            pltpu.SMEM((C,), jnp.int32),
            pltpu.VMEM((2, PAIR * R * L, P_SIZE), F32),
            pltpu.VMEM((C, L, R * HD), BF16),
            pltpu.VMEM((C, L, R * HD), BF16),
            pltpu.VMEM((2, TILES, R * HD, TILE), BF16),
            pltpu.VMEM((TILES, YN, 2, ROWS, TILE), BF16),
            pltpu.VMEM((TILES, 2, ROWS, TILE), BF16),
            pltpu.VMEM((TILES, 5, ROWS, TILE), BF16),
            pltpu.VMEM((ROWS, D), BF16),
            pltpu.VMEM((1, D), F32),
            pltpu.VMEM((ROWS, 128), F32),
            pltpu.VMEM((ROWS, 128), F32),
            dma((8,)), dma, dma, dma, dma((3,)), dma, dma((ZN,)), dma, dma((ZN,)),
            dma, dma, dma((2, ZN)), dma, dma, dma,
            dma, dma, dma, dma, dma, dma, dma((TILES,)), dma, dma, dma, dma((TILES,)),
        ],
        compiler_params=pltpu.CompilerParams(
            collective_id=0, has_side_effects=True, vmem_limit_bytes=VMEM_LIMIT
        ),
        cost_estimate=pl.CostEstimate(
            flops=2 * 2 * 64 * 128 * P_SIZE * HD + 2 * C * L * R * HD * D,
            bytes_accessed=16 << 20,
            transcendentals=8 << 20,
        ),
    )(group, lens, marks, q, ck, cv, pk, pv, residual, weight, head_w)


def local(
    cand_q, cand_k, cand_v, prompt_k, prompt_v, cand_group, cand_len, boundaries,
    residual, out_weight, head_weight,
):
    hidden, rewards = fused(
        cand_group,
        cand_len,
        boundaries.T,
        cand_q.reshape(C, L, R * HD),
        cand_k,
        cand_v,
        prompt_k,
        prompt_v,
        residual,
        out_weight,
        head_weight.reshape(1, D),
    )
    return hidden, rewards


def solution(mesh):
    in_specs = (
        P("dp", "tensor"),
        P("dp", "tensor"),
        P("dp", "tensor"),
        P("dp", "tensor"),
        P("dp", "tensor"),
        P("dp"),
        P("dp"),
        P("dp", None),
        P(("dp", "tensor"), None),
        P("tensor", None),
        P(),
    )
    out_specs = (P(("dp", "tensor"), None), P(("dp", "tensor"), None))
    return jax.shard_map(local, mesh=mesh, in_specs=in_specs, out_specs=out_specs, check_vma=False)
```

```python
import functools
import math

import jax
import jax.numpy as jnp
from jax import lax
from jax.experimental import pallas as pl
from jax.experimental.pallas import tpu as pltpu
from jax.sharding import PartitionSpec as P

HD = 128
P_SIZE = 1024
L = 32
C = 16
PAIR = 2
R = 4
XN, ZN, YN = 4, 8, 4
D = 8192
SCALE = 1.0 / math.sqrt(HD)
LOG2E = 1.4426950408889634
TILE = 512
TILES = D // 2 // TILE
AHEAD, BEHIND = 2, 4
ROWS = C * L // (2 * YN)
F32 = jnp.float32
BF16 = jnp.bfloat16
VMEM_LIMIT = 56 * 1024 * 1024


def remote(src, dst, send_sem, recv_sem, device):
    return pltpu.make_async_remote_copy(
        src_ref=src,
        dst_ref=dst,
        send_sem=send_sem,
        recv_sem=recv_sem,
        device_id=device,
        device_id_type=pl.DeviceIdType.MESH,
    )


def rows_of(block):
    return jnp.concatenate([block[:, r * HD : (r + 1) * HD] for r in range(R)], axis=0)


def with_ones(values):
    return jnp.concatenate([values, jnp.ones(values.shape, values.dtype)], axis=1)


def soften(scores, value_rows):
    highest = jnp.max(scores, axis=-1, keepdims=True)
    raised = jnp.exp2((scores - highest) * (SCALE * LOG2E)).astype(BF16)
    mixed = jnp.dot(raised, with_ones(value_rows), preferred_element_type=F32)
    summed = mixed[:, HD:]
    return mixed[:, :HD] / summed, highest * SCALE + jnp.log(summed)


def scores_of(queries, keys):
    return lax.dot_general(
        queries, keys, (((1,), (1,)), ((), ())), preferred_element_type=F32
    )


def fused_kernel(
    group_s, len_s, mark_s, q_in, ck_in, cv_in, pk, pv, residual_in, weight, head_in,
    hidden, rewards,
    qbuf, qfar, ck, cv, kbuf, vbuf, tabv, tabs, res, lsb, sfo, sfl, slot_s, scores,
    attn, attn_sib, wbuf, part, far, near, residual, head_w, squares, dots,
    loc_sem, tab_ss, tab_rs, q_ss, q_rs, k_ss, k_rs, v_ss, v_rs,
    ret_ss, ret_rs, lse_ss, lse_rs,
    w_sem, ws_ss, ws_rs, att_ss, att_rs, far_ss, far_rs, sib_ss, now_ss, late_ss, near_rs,
):
    dp = lax.axis_index("dp")
    x, z = dp // ZN, dp % ZN
    t = lax.axis_index("tensor")
    y, core = t // 2, t % 2

    def at(dp_at, t_at):
        return {"dp": dp_at, "tensor": t_at}

    xl = at(((x + XN - 1) % XN) * ZN + z, t)
    xr = at(((x + 1) % XN) * ZN + z, t)
    xx = at(((x + 2) % XN) * ZN + z, t)
    zl = at(x * ZN + (z + ZN - 1) % ZN, t)
    zr = at(x * ZN + (z + 1) % ZN, t)
    yr_at, yl_at, far_at = (y + 1) % YN, (y + YN - 1) % YN, (y + 2) % YN
    yr = [at(dp, yr_at * 2 + k) for k in range(2)]
    yl = [at(dp, yl_at * 2 + k) for k in range(2)]
    yr_same, yl_same = at(dp, yr_at * 2 + core), at(dp, yl_at * 2 + core)
    sibling = at(dp, y * 2 + 1 - core)

    barrier = pltpu.get_barrier_semaphore()
    peers = [zl, zr, xl, xr, xx, sibling] + yr + yl
    for device in peers:
        pl.semaphore_signal(
            barrier, inc=1, device_id=device, device_id_type=pl.DeviceIdType.MESH
        )

    pl.semaphore_wait(barrier, len(peers))

    def k_to(n, src, device):
        return remote(src, kbuf.at[n], k_ss, k_rs.at[n], device)

    def v_to(n, src, device):
        return remote(src, vbuf.at[n], v_ss, v_rs.at[n], device)

    k_to(1, pk, zr).start()
    k_to(2, pk, zl).start()
    half = C // 2
    lo, hi = pl.ds(0, half), pl.ds(half, half)

    def q_copy(sem, src, dst, device):
        return remote(src, dst, q_ss, q_rs.at[sem], device)

    def q_half(region, half_at):
        return qbuf.at[pl.ds(region * C + half_at * half, half)]

    q_copies = [
        q_copy(0, q_in.at[lo], q_half(1, 0), xr),
        q_copy(1, q_in.at[hi], q_half(2, 1), xl),
        q_copy(2, q_in.at[hi], q_half(1, 1), xr),
        q_copy(2, q_in.at[lo], q_half(2, 0), xl),
        q_copy(3, q_half(1, 0), qfar.at[lo], xr),
        q_copy(3, q_half(2, 1), qfar.at[hi], xl),
    ]
    q_copies[0].start()
    q_copies[1].start()
    v_to(1, pv, zr).start()
    v_to(2, pv, zl).start()
    q_copies[2].start()
    q_copies[3].start()
    own_k = pltpu.make_async_copy(pk, kbuf.at[0], loc_sem.at[0])
    own_v = pltpu.make_async_copy(pv, vbuf.at[0], loc_sem.at[1])
    own_q = pltpu.make_async_copy(q_in, qbuf.at[pl.ds(0, C)], loc_sem.at[2])
    own_ck = pltpu.make_async_copy(ck_in, ck, loc_sem.at[4])
    own_cv = pltpu.make_async_copy(cv_in, cv, loc_sem.at[5])
    for copy in (own_q, own_ck, own_cv, own_k, own_v):
        copy.start()
    groups = [group_s[c] for c in range(C)]
    lane = lax.broadcasted_iota(jnp.int32, (8, 128), 1)
    table = jnp.zeros((8, 128), jnp.int32)
    for c in range(C):
        slot = jnp.int32(0)
        for e in range(c):
            slot = slot + jnp.where(groups[e] == groups[c], 1, 0)
        slot = jnp.minimum(slot, PAIR - 1)
        table = jnp.where(lane == groups[c] * PAIR + slot, c, table)
        away = (groups[c] // ZN - x + XN) % XN
        region = jnp.where(away == 0, 0, jnp.where(away == 3, 4, jnp.where(away == 1, 5, 6)))
        back = (z - groups[c] % ZN + ZN) % ZN
        order = jnp.where(back == 0, 0, jnp.where(back <= 4, 2 * back - 1, 2 * (ZN - back)))
        slot_s[c] = region * C + order * PAIR + slot
    tabv[0] = table
    tab_copies = [
        remote(tabv.at[0], tabv.at[1], tab_ss, tab_rs, xr),
        remote(tabv.at[0], tabv.at[2], tab_ss, tab_rs, xl),
        remote(tabv.at[0], tabv.at[3], tab_ss, tab_rs, xx),
    ]
    for copy in tab_copies:
        copy.start()

    def w_columns(side, i):
        return weight.at[:, pl.ds(pl.multiple_of(side * (D // 2) + i * TILE, TILE), TILE)]

    def w_copy(i):
        return pltpu.make_async_copy(w_columns(core, i), wbuf.at[0, i], w_sem)

    def w_send(i):
        return remote(w_columns(1 - core, i), wbuf.at[1, i], ws_ss, ws_rs, sibling)

    def w_start(i, carry):
        w_copy(i).start()
        w_send(i).start()
        return carry

    lax.fori_loop(0, TILES, w_start, 0)
    res_copy = pltpu.make_async_copy(residual_in, residual, loc_sem.at[6])
    head_copy = pltpu.make_async_copy(head_in, head_w, loc_sem.at[7])
    res_copy.start()
    head_copy.start()

    own_q.wait()
    own_ck.wait()
    own_cv.wait()
    row = lax.broadcasted_iota(jnp.int32, (4 * R * L, 4 * L), 0)
    col = lax.broadcasted_iota(jnp.int32, (4 * R * L, 4 * L), 1)
    allowed = (row // (R * L) == col // L) & (col % L <= row % L)

    def suffix(g, carry):
        queries = jnp.concatenate([rows_of(qbuf[g * 4 + k]) for k in range(4)], axis=0)
        keys = ck[pl.ds(g * 4 * L, 4 * L), :]
        own_scores = jnp.where(allowed, scores_of(queries, keys), -1e30)
        mixed, lse = soften(own_scores, cv[pl.ds(g * 4 * L, 4 * L), :])
        for k in range(4):
            sfo[g * 4 + k] = mixed[k * R * L : (k + 1) * R * L]
            sfl[g * 4 + k] = lse[k * R * L : (k + 1) * R * L]
        return carry

    lax.fori_loop(0, C // 4, suffix, 0)

    q_copies[0].wait_recv()
    q_copies[4].start()
    q_copies[1].wait_recv()
    q_copies[5].start()
    own_k.wait()
    own_v.wait()
    for n, device in ((1, zr), (2, zl)):
        k_to(n, kbuf.at[n], device).wait_recv()
        k_to(n + 2, kbuf.at[n], device).start()
    for n, device in ((1, zr), (2, zl)):
        v_to(n, vbuf.at[n], device).wait_recv()
        v_to(n + 2, vbuf.at[n], device).start()
    tab_all = remote(tabv.at[pl.ds(1, 3)], tabv.at[pl.ds(1, 3)], tab_ss, tab_rs, xl)
    tab_all.wait_recv()
    to_smem = pltpu.make_async_copy(tabv, tabs, loc_sem.at[3])
    to_smem.start()
    remote(qfar, qfar, q_ss, q_rs.at[2], xl).wait_recv()
    to_smem.wait()

    eye = lax.broadcasted_iota(jnp.int32, (HD, HD), 0) == lax.broadcasted_iota(
        jnp.int32, (HD, HD), 1
    )

    def pair_at(region, n):
        return pl.ds(region * C + n * PAIR, PAIR)

    homes = {1: (5, xl), 2: (4, xr), 3: (6, xx)}

    def send_back(s, n):
        region, device = homes[s]
        remote(res.at[pair_at(s, n)], res.at[pair_at(region, n)], ret_ss, ret_rs, device).start()

    def two_sources(n, sources):
        owner_z = (z + (1 - 2 * (n % 2)) * ((n + 1) // 2) + ZN) % ZN
        base = (x * ZN + owner_z) * PAIR

        def queries_of(s):
            which = [tabs[s, 0, base + u] for u in range(PAIR)]
            blocks = [qfar[w] if s == 3 else qbuf[s * C + w] for w in which]
            return jnp.concatenate([rows_of(block) for block in blocks], axis=0)

        for k, s in enumerate(sources):
            scores[k] = scores_of(queries_of(s), kbuf[n])
        for k, s in enumerate(sources):
            mixed, lse = soften(scores[k], vbuf[n])
            mixed = mixed.astype(BF16)
            for u in range(PAIR):
                here = s * C + n * PAIR + u
                for r in range(R):
                    first = (u * R + r) * L
                    res[here, :, r * HD : (r + 1) * HD] = mixed[first : first + L]
                lsb[here] = jnp.sum(
                    jnp.where(eye, lse[u * HD : (u + 1) * HD], 0.0), axis=0, keepdims=True
                )
            if s:
                send_back(s, n)

    def step(h, carry):
        @pl.when(h == 3)
        def _():
            remote(qfar, qfar, q_ss, q_rs.at[3], xl).wait_recv()

        @pl.when(h == 4)
        def _():
            for m, device in ((3, zr), (4, zl)):
                k_to(m, kbuf.at[m], device).wait_recv()
                k_to(m + 2, kbuf.at[m], device).start()

        @pl.when(h == 6)
        def _():
            for m, device in ((3, zr), (4, zl)):
                v_to(m, vbuf.at[m], device).wait_recv()
                v_to(m + 2, vbuf.at[m], device).start()

        @pl.when(h == 8)
        def _():
            k_to(5, kbuf.at[5], zr).wait_recv()
            k_to(7, kbuf.at[5], zr).start()
            k_to(6, kbuf.at[6], zl).wait_recv()
            v_to(6, vbuf.at[6], zl).wait_recv()
            v_to(7, vbuf.at[6], zl).start()
            v_to(5, vbuf.at[5], zr).wait_recv()

        @pl.when(h == 10)
        def _():
            k_to(7, kbuf.at[5], zr).wait_recv()
            v_to(7, vbuf.at[6], zl).wait_recv()

        late_step = jnp.where(h < 3, 0, 1)

        @pl.when(h >= 3)
        def _():
            two_sources(h - 3 * late_step, (3, 0))

        @pl.when((h < 3) | (h >= 6))
        def _():
            two_sources(h - 3 * late_step, (1, 2))

        return carry

    lax.fori_loop(0, ZN + 3, step, 0)
    lse_copies = [
        remote(lsb.at[pl.ds(1 * C, C)], lsb.at[pl.ds(5 * C, C)], lse_ss, lse_rs, xl),
        remote(lsb.at[pl.ds(2 * C, C)], lsb.at[pl.ds(4 * C, C)], lse_ss, lse_rs, xr),
        remote(lsb.at[pl.ds(3 * C, C)], lsb.at[pl.ds(6 * C, C)], lse_ss, lse_rs, xx),
    ]
    for copy in lse_copies:
        copy.start()

    came = pl.ds(4 * C, 3 * C)
    res_all = remote(res.at[came], res.at[came], ret_ss, ret_rs, xl)
    lse_all = remote(lsb.at[came], lsb.at[came], lse_ss, lse_rs, xl)
    res_all.wait_recv()
    lse_all.wait_recv()

    def attn_copy(g, k):
        quarter = pl.ds(g * 4, 4)
        return remote(
            attn.at[quarter], attn_sib.at[quarter], att_ss, att_rs.at[(k + 2) // 3], sibling
        )

    def merge(k, carry):
        g = (y + jnp.where(k == 0, 2, jnp.where(k == 1, 1, jnp.where(k == 2, 3, 0)))) % YN
        for e in range(4):
            c = g * 4 + e
            where = slot_s[c]
            prefix = rows_of(res[where]).astype(F32)
            prefix_lse = jnp.sum(jnp.where(eye, lsb[where], 0.0), axis=1, keepdims=True)
            suffix_lse = sfl[c]
            largest = jnp.maximum(prefix_lse, suffix_lse)
            a = jnp.exp(prefix_lse - largest)
            b = jnp.exp(suffix_lse - largest)
            joined = ((a * prefix + b * sfo[c]) / (a + b)).astype(BF16)
            for r in range(R):
                attn[c, :, r * HD : (r + 1) * HD] = joined[r * L : (r + 1) * L]
        attn_copy(g, k).start()
        return carry

    lax.fori_loop(0, C // 4, merge, 0)

    squares[...] = jnp.zeros_like(squares)
    dots[...] = jnp.zeros_like(dots)

    def far_copies(i):
        return (
            remote(part.at[i, far_at, 0], far.at[i, 0], far_ss, far_rs.at[i], yr_same),
            remote(part.at[i, far_at, 1], far.at[i, 1], far_ss, far_rs.at[i], yl_same),
        )

    def now_copies(i):
        return (
            remote(part.at[i, yr_at, 1], near.at[i, core], now_ss, near_rs.at[i], yr[1]),
            remote(part.at[i, yl_at, 0], near.at[i, 2 + core], now_ss, near_rs.at[i], yl[0]),
        )

    def late_copies(i):
        return (
            remote(part.at[i, yr_at, 0], near.at[i, core], late_ss, near_rs.at[i], yr[0]),
            remote(part.at[i, yl_at, 1], near.at[i, 2 + core], late_ss, near_rs.at[i], yl[1]),
        )

    def sib_copy(i):
        return remote(part.at[i, y, 1 - core], near.at[i, 4], sib_ss, near_rs.at[i], sibling)

    def product(i, chunks):
        def rows(ref):
            blocks = [ref[pl.ds(g * 4, 4)].reshape(4 * L, R * HD) for g in chunks]
            return jnp.concatenate(blocks, axis=0)

        summed = jnp.dot(rows(attn), wbuf[0, i], preferred_element_type=F32) + jnp.dot(
            rows(attn_sib), wbuf[1, i], preferred_element_type=F32
        )
        for e, g in enumerate(chunks):
            block = summed[e * 4 * L : (e + 1) * 4 * L].astype(BF16)
            part[i, g] = block.reshape(2, ROWS, TILE)

    def multiply_far(i):
        product(i, (far_at,))
        for copy in far_copies(i):
            copy.start()

    def multiply_rest(i):
        product(i, (yr_at, yl_at, y))
        for copy in now_copies(i) + (sib_copy(i),):
            copy.start()

    def pass_on(i):
        late_r, late_l = late_copies(i)
        remote(far.at[i], far.at[i], far_ss, far_rs.at[i], yr_same).wait_recv()
        part[i, yr_at, 0] = (part[i, yr_at, 0].astype(F32) + far[i, 0].astype(F32)).astype(BF16)
        late_r.start()
        part[i, yl_at, 1] = (part[i, yl_at, 1].astype(F32) + far[i, 1].astype(F32)).astype(BF16)
        late_l.start()

    token = lax.broadcasted_iota(jnp.int32, (ROWS, 1), 0)
    first_cand = t * 2
    live = (token % L) < jnp.where(token < L, len_s[first_cand], len_s[first_cand + 1])

    def finish(i):
        remote(near.at[i], near.at[i], now_ss, near_rs.at[i], yr_same).wait_recv()
        for side, kept in ((core, part[i, y, core]), (1 - core, near[i, 4])):
            columns = pl.ds(pl.multiple_of(side * (D // 2) + i * TILE, TILE), TILE)
            total = (
                residual[:, columns].astype(F32)
                + kept.astype(F32)
                + near[i, side].astype(F32)
                + near[i, 2 + side].astype(F32)
            )
            out = jnp.where(live, total, 0.0).astype(BF16)
            hidden[:, columns] = out
            v = out.astype(F32)
            sq = v * v
            pr = v * head_w[:, columns]
            squares[...] += functools.reduce(
                jnp.add, [sq[:, k * 128 : (k + 1) * 128] for k in range(TILE // 128)]
            )
            dots[...] += functools.reduce(
                jnp.add, [pr[:, k * 128 : (k + 1) * 128] for k in range(TILE // 128)]
            )

    pltpu.make_async_copy(wbuf.at[0], wbuf.at[0], w_sem).wait()
    w_all = remote(wbuf.at[1], wbuf.at[1], ws_ss, ws_rs, sibling)
    w_all.wait_recv()
    attn_all = remote(attn, attn_sib, att_ss, att_rs.at[0], sibling)
    attn_rest = remote(attn.at[pl.ds(0, 12)], attn_sib.at[pl.ds(0, 12)], att_ss, att_rs.at[1], sibling)
    attn_copy(far_at, 0).wait_recv()
    res_copy.wait()
    head_copy.wait()

    def all_sent():
        others = pl.ds(1, ZN - 1)
        for copy in (
            remote(kbuf.at[others], kbuf.at[others], k_ss, k_rs.at[0], zr),
            remote(vbuf.at[others], vbuf.at[others], v_ss, v_rs.at[0], zr),
            remote(qbuf, qbuf, q_ss, q_rs.at[0], xr),
            tab_all, res_all, lse_all, w_all, attn_all,
        ):
            copy.wait_send()

    def tile_step(i, carry):
        @pl.when(i < TILES)
        def _():
            multiply_far(i)

        @pl.when(i == TILES)
        def _():
            all_sent()

        @pl.when(i == 1)
        def _():
            attn_rest.wait_recv()

        @pl.when((i >= 1) & (i < TILES + 1))
        def _():
            multiply_rest(i - 1)

        @pl.when((i >= AHEAD) & (i < TILES + AHEAD))
        def _():
            pass_on(i - AHEAD)

        @pl.when(i >= BEHIND)
        def _():
            finish(i - BEHIND)

        return carry

    lax.fori_loop(0, TILES + BEHIND, tile_step, 0)
    tiles = near.at[:, pl.ds(0, 2)]
    for sem in (far_ss, now_ss, late_ss):
        remote(tiles, tiles, sem, near_rs.at[0], yr_same).wait_send()
    remote(far.at[:, 0], far.at[:, 0], sib_ss, near_rs.at[0], sibling).wait_send()

    mean = jnp.sum(squares[...], axis=1, keepdims=True) * (1.0 / D)
    logit = jnp.sum(dots[...], axis=1, keepdims=True) * lax.rsqrt(mean + 1e-06)
    reward = 1.0 / (1.0 + jnp.exp(-logit))
    lane_row = lax.broadcasted_iota(jnp.int32, (1, 128), 1)
    for a in range(2):
        wanted = jnp.full((1, 128), -1, jnp.int32)
        for k in range(4):
            wanted = jnp.where(lane_row == k, a * L + mark_s[k, first_cand + a], wanted)
        picked = jnp.sum(jnp.where(token == wanted, reward, 0.0), axis=0, keepdims=True)
        rewards[a : a + 1, :] = picked[:, :4]


def fused(group, lens, marks, q, ck, cv, pk, pv, residual, weight, head_w):
    dma = pltpu.SemaphoreType.DMA
    any_space = pl.BlockSpec(memory_space=pl.ANY)
    vmem = pl.BlockSpec(memory_space=pltpu.VMEM)
    smem = pl.BlockSpec(memory_space=pltpu.SMEM)
    return pl.pallas_call(
        fused_kernel,
        out_shape=(
            pltpu.VMEM((ROWS, D), BF16),
            pltpu.VMEM((2, 4), F32),
        ),
        in_specs=[smem] * 3 + [any_space] * 8,
        out_specs=(vmem, vmem),
        scratch_shapes=[
            pltpu.VMEM((3 * C, L, R * HD), BF16),
            pltpu.VMEM((C, L, R * HD), BF16),
            pltpu.VMEM((C * L, HD), BF16),
            pltpu.VMEM((C * L, HD), BF16),
            pltpu.VMEM((ZN, P_SIZE, HD), BF16),
            pltpu.VMEM((ZN, P_SIZE, HD), BF16),
            pltpu.VMEM((XN, 8, 128), jnp.int32),
            pltpu.SMEM((XN, 8, 128), jnp.int32),
            pltpu.VMEM((7 * C, L, R * HD), BF16),
            pltpu.VMEM((7 * C, 1, HD), F32),
            pltpu.VMEM((C, R * L, HD), F32),
            pltpu.VMEM((C, R * L, HD), F32),
            pltpu.SMEM((C,), jnp.int32),
            pltpu.VMEM((2, PAIR * R * L, P_SIZE), F32),
            pltpu.VMEM((C, L, R * HD), BF16),
            pltpu.VMEM((C, L, R * HD), BF16),
            pltpu.VMEM((2, TILES, R * HD, TILE), BF16),
            pltpu.VMEM((TILES, YN, 2, ROWS, TILE), BF16),
            pltpu.VMEM((TILES, 2, ROWS, TILE), BF16),
            pltpu.VMEM((TILES, 5, ROWS, TILE), BF16),
            pltpu.VMEM((ROWS, D), BF16),
            pltpu.VMEM((1, D), F32),
            pltpu.VMEM((ROWS, 128), F32),
            pltpu.VMEM((ROWS, 128), F32),
            dma((8,)), dma, dma, dma, dma((4,)), dma, dma((ZN,)), dma, dma((ZN,)),
            dma, dma, dma, dma,
            dma, dma, dma, dma, dma((2,)), dma, dma((TILES,)), dma, dma, dma, dma((TILES,)),
        ],
        compiler_params=pltpu.CompilerParams(
            collective_id=0, has_side_effects=True, vmem_limit_bytes=VMEM_LIMIT
        ),
        cost_estimate=pl.CostEstimate(
            flops=2 * 2 * 64 * 128 * P_SIZE * HD + 2 * C * L * R * HD * D,
            bytes_accessed=16 << 20,
            transcendentals=8 << 20,
        ),
    )(group, lens, marks, q, ck, cv, pk, pv, residual, weight, head_w)


def local(
    cand_q, cand_k, cand_v, prompt_k, prompt_v, cand_group, cand_len, boundaries,
    residual, out_weight, head_weight,
):
    hidden, rewards = fused(
        cand_group,
        cand_len,
        boundaries.T,
        cand_q.reshape(C, L, R * HD),
        cand_k,
        cand_v,
        prompt_k,
        prompt_v,
        residual,
        out_weight,
        head_weight.reshape(1, D),
    )
    return hidden, rewards


def solution(mesh):
    in_specs = (
        P("dp", "tensor"),
        P("dp", "tensor"),
        P("dp", "tensor"),
        P("dp", "tensor"),
        P("dp", "tensor"),
        P("dp"),
        P("dp"),
        P("dp", None),
        P(("dp", "tensor"), None),
        P("tensor", None),
        P(),
    )
    out_specs = (P(("dp", "tensor"), None), P(("dp", "tensor"), None))
    return jax.shard_map(local, mesh=mesh, in_specs=in_specs, out_specs=out_specs, check_vma=False)
```

```python
import functools
import math

import jax
import jax.numpy as jnp
from jax import lax
from jax.experimental import pallas as pl
from jax.experimental.pallas import tpu as pltpu
from jax.sharding import PartitionSpec as P

HD = 128
P_SIZE = 1024
L = 32
C = 16
PAIR = 2
R = 4
XN, ZN, YN = 4, 8, 4
D = 8192
SCALE = 1.0 / math.sqrt(HD)
LOG2E = 1.4426950408889634
TILE = 512
TILES = D // 2 // TILE
AHEAD, BEHIND = 2, 4
ROWS = C * L // (2 * YN)
F32 = jnp.float32
BF16 = jnp.bfloat16
VMEM_LIMIT = 56 * 1024 * 1024


def remote(src, dst, send_sem, recv_sem, device):
    return pltpu.make_async_remote_copy(
        src_ref=src,
        dst_ref=dst,
        send_sem=send_sem,
        recv_sem=recv_sem,
        device_id=device,
        device_id_type=pl.DeviceIdType.MESH,
    )


def rows_of(block):
    return jnp.concatenate([block[:, r * HD : (r + 1) * HD] for r in range(R)], axis=0)


def with_ones(values):
    return jnp.concatenate([values, jnp.ones(values.shape, values.dtype)], axis=1)


def soften(scores, value_rows):
    highest = jnp.max(scores, axis=-1, keepdims=True)
    raised = jnp.exp2((scores - highest) * (SCALE * LOG2E)).astype(BF16)
    mixed = jnp.dot(raised, with_ones(value_rows), preferred_element_type=F32)
    summed = mixed[:, HD:]
    return mixed[:, :HD] / summed, highest * SCALE + jnp.log(summed)


def scores_of(queries, keys):
    return lax.dot_general(
        queries, keys, (((1,), (1,)), ((), ())), preferred_element_type=F32
    )


def fused_kernel(
    group_s, len_s, mark_s, q_in, ck_in, cv_in, pk, pv, residual_in, weight, head_in,
    hidden, rewards,
    qbuf, qfar, ck, cv, kbuf, vbuf, tabv, tabs, res, lsb, sfo, sfl, slot_s, scores,
    attn, attn_sib, wbuf, part, far, near, residual, head_w, squares, dots,
    loc_sem, tab_ss, tab_rs, q_ss, q_rs, k_ss, k_rs, v_ss, v_rs,
    ret_ss, ret_rs, lse_ss, lse_rs,
    w_sem, ws_ss, ws_rs, att_ss, att_rs, far_ss, far_rs, sib_ss, now_ss, late_ss, near_rs,
):
    dp = lax.axis_index("dp")
    x, z = dp // ZN, dp % ZN
    t = lax.axis_index("tensor")
    y, core = t // 2, t % 2

    def at(dp_at, t_at):
        return {"dp": dp_at, "tensor": t_at}

    xl = at(((x + XN - 1) % XN) * ZN + z, t)
    xr = at(((x + 1) % XN) * ZN + z, t)
    xx = at(((x + 2) % XN) * ZN + z, t)
    zl = at(x * ZN + (z + ZN - 1) % ZN, t)
    zr = at(x * ZN + (z + 1) % ZN, t)
    yr_at, yl_at, far_at = (y + 1) % YN, (y + YN - 1) % YN, (y + 2) % YN
    yr = [at(dp, yr_at * 2 + k) for k in range(2)]
    yl = [at(dp, yl_at * 2 + k) for k in range(2)]
    yr_same, yl_same = at(dp, yr_at * 2 + core), at(dp, yl_at * 2 + core)
    sibling = at(dp, y * 2 + 1 - core)

    barrier = pltpu.get_barrier_semaphore()
    peers = [zl, zr, xl, xr, xx, sibling] + yr + yl
    for device in peers:
        pl.semaphore_signal(
            barrier, inc=1, device_id=device, device_id_type=pl.DeviceIdType.MESH
        )

    pl.semaphore_wait(barrier, len(peers))

    def k_to(n, src, device):
        return remote(src, kbuf.at[n], k_ss, k_rs.at[n], device)

    def v_to(n, src, device):
        return remote(src, vbuf.at[n], v_ss, v_rs.at[n], device)

    k_to(1, pk, zr).start()
    k_to(2, pk, zl).start()
    half = C // 2
    lo, hi = pl.ds(0, half), pl.ds(half, half)

    def q_copy(sem, src, dst, device):
        return remote(src, dst, q_ss, q_rs.at[sem], device)

    def q_half(region, half_at):
        return qbuf.at[pl.ds(region * C + half_at * half, half)]

    q_copies = [
        q_copy(0, q_in.at[lo], q_half(1, 0), xr),
        q_copy(1, q_in.at[hi], q_half(2, 1), xl),
        q_copy(2, q_in.at[hi], q_half(1, 1), xr),
        q_copy(2, q_in.at[lo], q_half(2, 0), xl),
        q_copy(3, q_half(1, 0), qfar.at[lo], xr),
        q_copy(3, q_half(2, 1), qfar.at[hi], xl),
    ]
    q_copies[0].start()
    q_copies[1].start()
    v_to(1, pv, zr).start()
    v_to(2, pv, zl).start()
    q_copies[2].start()
    q_copies[3].start()
    own_k = pltpu.make_async_copy(pk, kbuf.at[0], loc_sem.at[0])
    own_v = pltpu.make_async_copy(pv, vbuf.at[0], loc_sem.at[1])
    own_q = pltpu.make_async_copy(q_in, qbuf.at[pl.ds(0, C)], loc_sem.at[2])
    own_ck = pltpu.make_async_copy(ck_in, ck, loc_sem.at[4])
    own_cv = pltpu.make_async_copy(cv_in, cv, loc_sem.at[5])
    for copy in (own_q, own_ck, own_cv, own_k, own_v):
        copy.start()
    groups = [group_s[c] for c in range(C)]
    lane = lax.broadcasted_iota(jnp.int32, (8, 128), 1)
    table = jnp.zeros((8, 128), jnp.int32)
    for c in range(C):
        slot = jnp.int32(0)
        for e in range(c):
            slot = slot + jnp.where(groups[e] == groups[c], 1, 0)
        slot = jnp.minimum(slot, PAIR - 1)
        table = jnp.where(lane == groups[c] * PAIR + slot, c, table)
        away = (groups[c] // ZN - x + XN) % XN
        region = jnp.where(away == 0, 0, jnp.where(away == 3, 4, jnp.where(away == 1, 5, 6)))
        back = (z - groups[c] % ZN + ZN) % ZN
        order = jnp.where(back == 0, 0, jnp.where(back <= 4, 2 * back - 1, 2 * (ZN - back)))
        slot_s[c] = region * C + order * PAIR + slot
    tabv[0] = table
    tab_copies = [
        remote(tabv.at[0], tabv.at[1], tab_ss, tab_rs, xr),
        remote(tabv.at[0], tabv.at[2], tab_ss, tab_rs, xl),
        remote(tabv.at[0], tabv.at[3], tab_ss, tab_rs, xx),
    ]
    for copy in tab_copies:
        copy.start()

    def w_columns(side, i):
        return weight.at[:, pl.ds(pl.multiple_of(side * (D // 2) + i * TILE, TILE), TILE)]

    def w_copy(i):
        return pltpu.make_async_copy(w_columns(core, i), wbuf.at[0, i], w_sem)

    def w_send(i):
        return remote(w_columns(1 - core, i), wbuf.at[1, i], ws_ss, ws_rs, sibling)

    def w_start(i, carry):
        w_copy(i).start()
        w_send(i).start()
        return carry

    lax.fori_loop(0, TILES, w_start, 0)
    res_copy = pltpu.make_async_copy(residual_in, residual, loc_sem.at[6])
    head_copy = pltpu.make_async_copy(head_in, head_w, loc_sem.at[7])
    res_copy.start()
    head_copy.start()

    own_q.wait()
    own_ck.wait()
    own_cv.wait()
    row = lax.broadcasted_iota(jnp.int32, (4 * R * L, 4 * L), 0)
    col = lax.broadcasted_iota(jnp.int32, (4 * R * L, 4 * L), 1)
    allowed = (row // (R * L) == col // L) & (col % L <= row % L)

    def suffix(g, carry):
        queries = jnp.concatenate([rows_of(qbuf[g * 4 + k]) for k in range(4)], axis=0)
        keys = ck[pl.ds(g * 4 * L, 4 * L), :]
        own_scores = jnp.where(allowed, scores_of(queries, keys), -1e30)
        mixed, lse = soften(own_scores, cv[pl.ds(g * 4 * L, 4 * L), :])
        for k in range(4):
            sfo[g * 4 + k] = mixed[k * R * L : (k + 1) * R * L]
            sfl[g * 4 + k] = lse[k * R * L : (k + 1) * R * L]
        return carry

    lax.fori_loop(0, C // 4, suffix, 0)

    q_copies[0].wait_recv()
    q_copies[4].start()
    q_copies[1].wait_recv()
    q_copies[5].start()
    own_k.wait()
    own_v.wait()
    for n, device in ((1, zr), (2, zl)):
        k_to(n, kbuf.at[n], device).wait_recv()
        k_to(n + 2, kbuf.at[n], device).start()
    for n, device in ((1, zr), (2, zl)):
        v_to(n, vbuf.at[n], device).wait_recv()
        v_to(n + 2, vbuf.at[n], device).start()
    tab_all = remote(tabv.at[pl.ds(1, 3)], tabv.at[pl.ds(1, 3)], tab_ss, tab_rs, xl)
    tab_all.wait_recv()
    to_smem = pltpu.make_async_copy(tabv, tabs, loc_sem.at[3])
    to_smem.start()
    remote(qfar, qfar, q_ss, q_rs.at[2], xl).wait_recv()
    to_smem.wait()

    eye = lax.broadcasted_iota(jnp.int32, (HD, HD), 0) == lax.broadcasted_iota(
        jnp.int32, (HD, HD), 1
    )

    def pair_at(region, n):
        return pl.ds(region * C + n * PAIR, PAIR)

    homes = {1: (5, xl), 2: (4, xr), 3: (6, xx)}

    def send_back(s, n):
        region, device = homes[s]
        remote(res.at[pair_at(s, n)], res.at[pair_at(region, n)], ret_ss, ret_rs, device).start()

    def form_scores(n, sources):
        owner_z = (z + (1 - 2 * (n % 2)) * ((n + 1) // 2) + ZN) % ZN
        base = (x * ZN + owner_z) * PAIR

        def queries_of(s):
            which = [tabs[s, 0, base + u] for u in range(PAIR)]
            blocks = [qfar[w] if s == 3 else qbuf[s * C + w] for w in which]
            return jnp.concatenate([rows_of(block) for block in blocks], axis=0)

        for k, s in enumerate(sources):
            scores[k] = scores_of(queries_of(s), kbuf[n])

    def settle(n, sources):
        for k, s in enumerate(sources):
            mixed, lse = soften(scores[k], vbuf[n])
            mixed = mixed.astype(BF16)
            for u in range(PAIR):
                here = s * C + n * PAIR + u
                for r in range(R):
                    first = (u * R + r) * L
                    res[here, :, r * HD : (r + 1) * HD] = mixed[first : first + L]
                lsb[here] = jnp.sum(
                    jnp.where(eye, lse[u * HD : (u + 1) * HD], 0.0), axis=0, keepdims=True
                )
            if s:
                send_back(s, n)

    def two_sources(n, sources):
        form_scores(n, sources)
        settle(n, sources)

    def last_halves(buf, send_sem, recv_sems):
        lower, upper = pl.ds(0, P_SIZE // 2), pl.ds(P_SIZE // 2, P_SIZE // 2)
        last = recv_sems.at[ZN - 1]
        return (
            remote(buf.at[5, lower], buf.at[7, lower], send_sem, last, zr),
            remote(buf.at[6, upper], buf.at[7, upper], send_sem, last, zl),
        )

    def step(h, carry):
        @pl.when(h == 3)
        def _():
            remote(qfar, qfar, q_ss, q_rs.at[3], xl).wait_recv()

        @pl.when(h == 4)
        def _():
            for m, device in ((3, zr), (4, zl)):
                k_to(m, kbuf.at[m], device).wait_recv()
                k_to(m + 2, kbuf.at[m], device).start()

        @pl.when(h == 6)
        def _():
            for m, device in ((3, zr), (4, zl)):
                v_to(m, vbuf.at[m], device).wait_recv()
                v_to(m + 2, vbuf.at[m], device).start()

        @pl.when(h == 8)
        def _():
            k_to(5, kbuf.at[5], zr).wait_recv()
            k_to(6, kbuf.at[6], zl).wait_recv()
            for copy in last_halves(kbuf, k_ss, k_rs):
                copy.start()
            v_to(5, vbuf.at[5], zr).wait_recv()
            v_to(6, vbuf.at[6], zl).wait_recv()
            for copy in last_halves(vbuf, v_ss, v_rs):
                copy.start()

        late_step = jnp.where(h < 3, 0, 1)

        @pl.when(h >= 3)
        def _():
            two_sources(h - 3 * late_step, (3, 0))

        @pl.when((h < 3) | (h >= 6))
        def _():
            two_sources(h - 3 * late_step, (1, 2))

        return carry

    lax.fori_loop(0, ZN + 2, step, 0)
    k_to(7, kbuf.at[7], zr).wait_recv()
    form_scores(ZN - 1, (3, 1, 2, 0))
    v_to(7, vbuf.at[7], zr).wait_recv()
    settle(ZN - 1, (3, 1, 2, 0))
    lse_copies = [
        remote(lsb.at[pl.ds(1 * C, C)], lsb.at[pl.ds(5 * C, C)], lse_ss, lse_rs, xl),
        remote(lsb.at[pl.ds(2 * C, C)], lsb.at[pl.ds(4 * C, C)], lse_ss, lse_rs, xr),
        remote(lsb.at[pl.ds(3 * C, C)], lsb.at[pl.ds(6 * C, C)], lse_ss, lse_rs, xx),
    ]
    for copy in lse_copies:
        copy.start()

    came = pl.ds(4 * C, 3 * C)
    res_all = remote(res.at[came], res.at[came], ret_ss, ret_rs, xl)
    lse_all = remote(lsb.at[came], lsb.at[came], lse_ss, lse_rs, xl)
    res_all.wait_recv()
    lse_all.wait_recv()

    def attn_copy(g, k):
        quarter = pl.ds(g * 4, 4)
        return remote(
            attn.at[quarter], attn_sib.at[quarter], att_ss, att_rs.at[(k + 2) // 3], sibling
        )

    def merge(k, carry):
        g = (y + jnp.where(k == 0, 2, jnp.where(k == 1, 1, jnp.where(k == 2, 3, 0)))) % YN
        for e in range(4):
            c = g * 4 + e
            where = slot_s[c]
            prefix = rows_of(res[where]).astype(F32)
            prefix_lse = jnp.sum(jnp.where(eye, lsb[where], 0.0), axis=1, keepdims=True)
            suffix_lse = sfl[c]
            largest = jnp.maximum(prefix_lse, suffix_lse)
            a = jnp.exp(prefix_lse - largest)
            b = jnp.exp(suffix_lse - largest)
            joined = ((a * prefix + b * sfo[c]) / (a + b)).astype(BF16)
            for r in range(R):
                attn[c, :, r * HD : (r + 1) * HD] = joined[r * L : (r + 1) * L]
        attn_copy(g, k).start()
        return carry

    lax.fori_loop(0, C // 4, merge, 0)

    squares[...] = jnp.zeros_like(squares)
    dots[...] = jnp.zeros_like(dots)

    def far_copies(i):
        return (
            remote(part.at[i, far_at, 0], far.at[i, 0], far_ss, far_rs.at[i], yr_same),
            remote(part.at[i, far_at, 1], far.at[i, 1], far_ss, far_rs.at[i], yl_same),
        )

    def now_copies(i):
        return (
            remote(part.at[i, yr_at, 1], near.at[i, core], now_ss, near_rs.at[i], yr[1]),
            remote(part.at[i, yl_at, 0], near.at[i, 2 + core], now_ss, near_rs.at[i], yl[0]),
        )

    def late_copies(i):
        return (
            remote(part.at[i, yr_at, 0], near.at[i, core], late_ss, near_rs.at[i], yr[0]),
            remote(part.at[i, yl_at, 1], near.at[i, 2 + core], late_ss, near_rs.at[i], yl[1]),
        )

    def sib_copy(i):
        return remote(part.at[i, y, 1 - core], near.at[i, 4], sib_ss, near_rs.at[i], sibling)

    def product(i, chunks):
        def rows(ref):
            blocks = [ref[pl.ds(g * 4, 4)].reshape(4 * L, R * HD) for g in chunks]
            return jnp.concatenate(blocks, axis=0)

        summed = jnp.dot(rows(attn), wbuf[0, i], preferred_element_type=F32) + jnp.dot(
            rows(attn_sib), wbuf[1, i], preferred_element_type=F32
        )
        for e, g in enumerate(chunks):
            block = summed[e * 4 * L : (e + 1) * 4 * L].astype(BF16)
            part[i, g] = block.reshape(2, ROWS, TILE)

    def multiply_far(i):
        product(i, (far_at,))
        for copy in far_copies(i):
            copy.start()

    def multiply_rest(i):
        product(i, (yr_at, yl_at, y))
        for copy in now_copies(i) + (sib_copy(i),):
            copy.start()

    def pass_on(i):
        late_r, late_l = late_copies(i)
        remote(far.at[i], far.at[i], far_ss, far_rs.at[i], yr_same).wait_recv()
        part[i, yr_at, 0] = (part[i, yr_at, 0].astype(F32) + far[i, 0].astype(F32)).astype(BF16)
        late_r.start()
        part[i, yl_at, 1] = (part[i, yl_at, 1].astype(F32) + far[i, 1].astype(F32)).astype(BF16)
        late_l.start()

    token = lax.broadcasted_iota(jnp.int32, (ROWS, 1), 0)
    first_cand = t * 2
    live = (token % L) < jnp.where(token < L, len_s[first_cand], len_s[first_cand + 1])

    def finish(i):
        remote(near.at[i], near.at[i], now_ss, near_rs.at[i], yr_same).wait_recv()
        for side, kept in ((core, part[i, y, core]), (1 - core, near[i, 4])):
            columns = pl.ds(pl.multiple_of(side * (D // 2) + i * TILE, TILE), TILE)
            total = (
                residual[:, columns].astype(F32)
                + kept.astype(F32)
                + near[i, side].astype(F32)
                + near[i, 2 + side].astype(F32)
            )
            out = jnp.where(live, total, 0.0).astype(BF16)
            hidden[:, columns] = out
            v = out.astype(F32)
            sq = v * v
            pr = v * head_w[:, columns]
            squares[...] += functools.reduce(
                jnp.add, [sq[:, k * 128 : (k + 1) * 128] for k in range(TILE // 128)]
            )
            dots[...] += functools.reduce(
                jnp.add, [pr[:, k * 128 : (k + 1) * 128] for k in range(TILE // 128)]
            )

    pltpu.make_async_copy(wbuf.at[0], wbuf.at[0], w_sem).wait()
    w_all = remote(wbuf.at[1], wbuf.at[1], ws_ss, ws_rs, sibling)
    w_all.wait_recv()
    attn_all = remote(attn, attn_sib, att_ss, att_rs.at[0], sibling)
    attn_rest = remote(attn.at[pl.ds(0, 12)], attn_sib.at[pl.ds(0, 12)], att_ss, att_rs.at[1], sibling)
    attn_copy(far_at, 0).wait_recv()
    res_copy.wait()
    head_copy.wait()

    def all_sent():
        others = pl.ds(1, ZN - 1)
        for copy in (
            remote(kbuf.at[others], kbuf.at[others], k_ss, k_rs.at[0], zr),
            remote(vbuf.at[others], vbuf.at[others], v_ss, v_rs.at[0], zr),
            remote(qbuf, qbuf, q_ss, q_rs.at[0], xr),
            tab_all, res_all, lse_all, w_all, attn_all,
        ):
            copy.wait_send()

    def tile_step(i, carry):
        @pl.when(i < TILES)
        def _():
            multiply_far(i)

        @pl.when(i == TILES)
        def _():
            all_sent()

        @pl.when(i == 1)
        def _():
            attn_rest.wait_recv()

        @pl.when((i >= 1) & (i < TILES + 1))
        def _():
            multiply_rest(i - 1)

        @pl.when((i >= AHEAD) & (i < TILES + AHEAD))
        def _():
            pass_on(i - AHEAD)

        @pl.when(i >= BEHIND)
        def _():
            finish(i - BEHIND)

        return carry

    lax.fori_loop(0, TILES + BEHIND, tile_step, 0)
    tiles = near.at[:, pl.ds(0, 2)]
    for sem in (far_ss, now_ss, late_ss):
        remote(tiles, tiles, sem, near_rs.at[0], yr_same).wait_send()
    remote(far.at[:, 0], far.at[:, 0], sib_ss, near_rs.at[0], sibling).wait_send()

    mean = jnp.sum(squares[...], axis=1, keepdims=True) * (1.0 / D)
    logit = jnp.sum(dots[...], axis=1, keepdims=True) * lax.rsqrt(mean + 1e-06)
    reward = 1.0 / (1.0 + jnp.exp(-logit))
    lane_row = lax.broadcasted_iota(jnp.int32, (1, 128), 1)
    for a in range(2):
        wanted = jnp.full((1, 128), -1, jnp.int32)
        for k in range(4):
            wanted = jnp.where(lane_row == k, a * L + mark_s[k, first_cand + a], wanted)
        picked = jnp.sum(jnp.where(token == wanted, reward, 0.0), axis=0, keepdims=True)
        rewards[a : a + 1, :] = picked[:, :4]


def fused(group, lens, marks, q, ck, cv, pk, pv, residual, weight, head_w):
    dma = pltpu.SemaphoreType.DMA
    any_space = pl.BlockSpec(memory_space=pl.ANY)
    vmem = pl.BlockSpec(memory_space=pltpu.VMEM)
    smem = pl.BlockSpec(memory_space=pltpu.SMEM)
    return pl.pallas_call(
        fused_kernel,
        out_shape=(
            pltpu.VMEM((ROWS, D), BF16),
            pltpu.VMEM((2, 4), F32),
        ),
        in_specs=[smem] * 3 + [any_space] * 8,
        out_specs=(vmem, vmem),
        scratch_shapes=[
            pltpu.VMEM((3 * C, L, R * HD), BF16),
            pltpu.VMEM((C, L, R * HD), BF16),
            pltpu.VMEM((C * L, HD), BF16),
            pltpu.VMEM((C * L, HD), BF16),
            pltpu.VMEM((ZN, P_SIZE, HD), BF16),
            pltpu.VMEM((ZN, P_SIZE, HD), BF16),
            pltpu.VMEM((XN, 8, 128), jnp.int32),
            pltpu.SMEM((XN, 8, 128), jnp.int32),
            pltpu.VMEM((7 * C, L, R * HD), BF16),
            pltpu.VMEM((7 * C, 1, HD), F32),
            pltpu.VMEM((C, R * L, HD), F32),
            pltpu.VMEM((C, R * L, HD), F32),
            pltpu.SMEM((C,), jnp.int32),
            pltpu.VMEM((XN, PAIR * R * L, P_SIZE), F32),
            pltpu.VMEM((C, L, R * HD), BF16),
            pltpu.VMEM((C, L, R * HD), BF16),
            pltpu.VMEM((2, TILES, R * HD, TILE), BF16),
            pltpu.VMEM((TILES, YN, 2, ROWS, TILE), BF16),
            pltpu.VMEM((TILES, 2, ROWS, TILE), BF16),
            pltpu.VMEM((TILES, 5, ROWS, TILE), BF16),
            pltpu.VMEM((ROWS, D), BF16),
            pltpu.VMEM((1, D), F32),
            pltpu.VMEM((ROWS, 128), F32),
            pltpu.VMEM((ROWS, 128), F32),
            dma((8,)), dma, dma, dma, dma((4,)), dma, dma((ZN,)), dma, dma((ZN,)),
            dma, dma, dma, dma,
            dma, dma, dma, dma, dma((2,)), dma, dma((TILES,)), dma, dma, dma, dma((TILES,)),
        ],
        compiler_params=pltpu.CompilerParams(
            collective_id=0, has_side_effects=True, vmem_limit_bytes=VMEM_LIMIT
        ),
        cost_estimate=pl.CostEstimate(
            flops=2 * 2 * 64 * 128 * P_SIZE * HD + 2 * C * L * R * HD * D,
            bytes_accessed=16 << 20,
            transcendentals=8 << 20,
        ),
    )(group, lens, marks, q, ck, cv, pk, pv, residual, weight, head_w)


def local(
    cand_q, cand_k, cand_v, prompt_k, prompt_v, cand_group, cand_len, boundaries,
    residual, out_weight, head_weight,
):
    hidden, rewards = fused(
        cand_group,
        cand_len,
        boundaries.T,
        cand_q.reshape(C, L, R * HD),
        cand_k,
        cand_v,
        prompt_k,
        prompt_v,
        residual,
        out_weight,
        head_weight.reshape(1, D),
    )
    return hidden, rewards


def solution(mesh):
    in_specs = (
        P("dp", "tensor"),
        P("dp", "tensor"),
        P("dp", "tensor"),
        P("dp", "tensor"),
        P("dp", "tensor"),
        P("dp"),
        P("dp"),
        P("dp", None),
        P(("dp", "tensor"), None),
        P("tensor", None),
        P(),
    )
    out_specs = (P(("dp", "tensor"), None), P(("dp", "tensor"), None))
    return jax.shard_map(local, mesh=mesh, in_specs=in_specs, out_specs=out_specs, check_vma=False)
```

```python
import functools
import math

import jax
import jax.numpy as jnp
from jax import lax
from jax.experimental import pallas as pl
from jax.experimental.pallas import tpu as pltpu
from jax.sharding import PartitionSpec as P

HD = 128
P_SIZE = 1024
L = 32
C = 16
PAIR = 2
R = 4
XN, ZN, YN = 4, 8, 4
D = 8192
SCALE = 1.0 / math.sqrt(HD)
LOG2E = 1.4426950408889634
TILE = 512
TILES = D // 2 // TILE
AHEAD, BEHIND = 2, 4
ROWS = C * L // (2 * YN)
F32 = jnp.float32
BF16 = jnp.bfloat16
VMEM_LIMIT = 56 * 1024 * 1024


def remote(src, dst, send_sem, recv_sem, device):
    return pltpu.make_async_remote_copy(
        src_ref=src,
        dst_ref=dst,
        send_sem=send_sem,
        recv_sem=recv_sem,
        device_id=device,
        device_id_type=pl.DeviceIdType.MESH,
    )


def rows_of(block):
    return jnp.concatenate([block[:, r * HD : (r + 1) * HD] for r in range(R)], axis=0)


def with_ones(values):
    return jnp.concatenate([values, jnp.ones(values.shape, values.dtype)], axis=1)


def soften(scores, value_rows):
    highest = jnp.max(scores, axis=-1, keepdims=True)
    raised = jnp.exp2((scores - highest) * (SCALE * LOG2E)).astype(BF16)
    mixed = jnp.dot(raised, with_ones(value_rows), preferred_element_type=F32)
    summed = mixed[:, HD:]
    return mixed[:, :HD] / summed, highest * SCALE + jnp.log(summed)


def scores_of(queries, keys):
    return lax.dot_general(
        queries, keys, (((1,), (1,)), ((), ())), preferred_element_type=F32
    )


def fused_kernel(
    group_s, len_s, mark_s, q_in, ck_in, cv_in, pk, pv, residual_in, weight, head_in,
    hidden, rewards,
    qbuf, qfar, ck, cv, kbuf, vbuf, tabv, tabs, res, lsb, sfo, sfl, slot_s, scores,
    attn, attn_sib, wbuf, part, far, near, residual, head_w, squares, dots,
    loc_sem, tab_ss, tab_rs, q_ss, q_rs, k_ss, k_rs, v_ss, v_rs,
    ret_ss, ret_rs, lse_ss, lse_rs,
    w_sem, ws_ss, ws_rs, att_ss, att_rs, far_ss, far_rs, sib_ss, now_ss, late_ss, near_rs,
):
    dp = lax.axis_index("dp")
    x, z = dp // ZN, dp % ZN
    t = lax.axis_index("tensor")
    y, core = t // 2, t % 2

    def at(dp_at, t_at):
        return {"dp": dp_at, "tensor": t_at}

    xl = at(((x + XN - 1) % XN) * ZN + z, t)
    xr = at(((x + 1) % XN) * ZN + z, t)
    xx = at(((x + 2) % XN) * ZN + z, t)
    zl = at(x * ZN + (z + ZN - 1) % ZN, t)
    zr = at(x * ZN + (z + 1) % ZN, t)
    yr_at, yl_at, far_at = (y + 1) % YN, (y + YN - 1) % YN, (y + 2) % YN
    yr = [at(dp, yr_at * 2 + k) for k in range(2)]
    yl = [at(dp, yl_at * 2 + k) for k in range(2)]
    yr_same, yl_same = at(dp, yr_at * 2 + core), at(dp, yl_at * 2 + core)
    sibling = at(dp, y * 2 + 1 - core)

    barrier = pltpu.get_barrier_semaphore()
    peers = [zl, zr, xl, xr, xx, sibling] + yr + yl
    for device in peers:
        pl.semaphore_signal(
            barrier, inc=1, device_id=device, device_id_type=pl.DeviceIdType.MESH
        )

    pl.semaphore_wait(barrier, len(peers))

    def k_to(n, src, device):
        return remote(src, kbuf.at[n], k_ss, k_rs.at[n], device)

    def v_to(n, src, device):
        return remote(src, vbuf.at[n], v_ss, v_rs.at[n], device)

    k_to(1, pk, zr).start()
    k_to(2, pk, zl).start()
    half = C // 2
    lo, hi = pl.ds(0, half), pl.ds(half, half)

    def q_copy(sem, src, dst, device):
        return remote(src, dst, q_ss, q_rs.at[sem], device)

    def q_half(region, half_at):
        return qbuf.at[pl.ds(region * C + half_at * half, half)]

    q_copies = [
        q_copy(0, q_in.at[lo], q_half(1, 0), xr),
        q_copy(1, q_in.at[hi], q_half(2, 1), xl),
        q_copy(2, q_in.at[hi], q_half(1, 1), xr),
        q_copy(2, q_in.at[lo], q_half(2, 0), xl),
        q_copy(3, q_half(1, 0), qfar.at[lo], xr),
        q_copy(3, q_half(2, 1), qfar.at[hi], xl),
    ]
    q_copies[0].start()
    q_copies[1].start()
    v_to(1, pv, zr).start()
    v_to(2, pv, zl).start()
    q_copies[2].start()
    q_copies[3].start()
    own_k = pltpu.make_async_copy(pk, kbuf.at[0], loc_sem.at[0])
    own_v = pltpu.make_async_copy(pv, vbuf.at[0], loc_sem.at[1])
    own_q = pltpu.make_async_copy(q_in, qbuf.at[pl.ds(0, C)], loc_sem.at[2])
    own_ck = pltpu.make_async_copy(ck_in, ck, loc_sem.at[4])
    own_cv = pltpu.make_async_copy(cv_in, cv, loc_sem.at[5])
    for copy in (own_q, own_ck, own_cv, own_k, own_v):
        copy.start()
    groups = [group_s[c] for c in range(C)]
    lane = lax.broadcasted_iota(jnp.int32, (8, 128), 1)
    table = jnp.zeros((8, 128), jnp.int32)
    for c in range(C):
        slot = jnp.int32(0)
        for e in range(c):
            slot = slot + jnp.where(groups[e] == groups[c], 1, 0)
        slot = jnp.minimum(slot, PAIR - 1)
        table = jnp.where(lane == groups[c] * PAIR + slot, c, table)
        away = (groups[c] // ZN - x + XN) % XN
        region = jnp.where(away == 0, 0, jnp.where(away == 3, 4, jnp.where(away == 1, 5, 6)))
        back = (z - groups[c] % ZN + ZN) % ZN
        order = jnp.where(back == 0, 0, jnp.where(back <= 4, 2 * back - 1, 2 * (ZN - back)))
        slot_s[c] = region * C + order * PAIR + slot
    tabv[0] = table
    tab_copies = [
        remote(tabv.at[0], tabv.at[1], tab_ss, tab_rs, xr),
        remote(tabv.at[0], tabv.at[2], tab_ss, tab_rs, xl),
        remote(tabv.at[0], tabv.at[3], tab_ss, tab_rs, xx),
    ]
    for copy in tab_copies:
        copy.start()

    def w_columns(side, i):
        return weight.at[:, pl.ds(pl.multiple_of(side * (D // 2) + i * TILE, TILE), TILE)]

    def w_copy(i):
        return pltpu.make_async_copy(w_columns(core, i), wbuf.at[0, i], w_sem)

    def w_send(i):
        return remote(w_columns(1 - core, i), wbuf.at[1, i], ws_ss, ws_rs, sibling)

    def w_start(i, carry):
        w_copy(i).start()
        w_send(i).start()
        return carry

    lax.fori_loop(0, TILES, w_start, 0)
    res_copy = pltpu.make_async_copy(residual_in, residual, loc_sem.at[6])
    head_copy = pltpu.make_async_copy(head_in, head_w, loc_sem.at[7])
    res_copy.start()
    head_copy.start()

    own_q.wait()
    own_ck.wait()
    own_cv.wait()
    row = lax.broadcasted_iota(jnp.int32, (4 * R * L, 4 * L), 0)
    col = lax.broadcasted_iota(jnp.int32, (4 * R * L, 4 * L), 1)
    allowed = (row // (R * L) == col // L) & (col % L <= row % L)

    def suffix(g, carry):
        queries = jnp.concatenate([rows_of(qbuf[g * 4 + k]) for k in range(4)], axis=0)
        keys = ck[pl.ds(g * 4 * L, 4 * L), :]
        own_scores = jnp.where(allowed, scores_of(queries, keys), -1e30)
        mixed, lse = soften(own_scores, cv[pl.ds(g * 4 * L, 4 * L), :])
        for k in range(4):
            sfo[g * 4 + k] = mixed[k * R * L : (k + 1) * R * L]
            sfl[g * 4 + k] = lse[k * R * L : (k + 1) * R * L]
        return carry

    lax.fori_loop(0, C // 4, suffix, 0)

    q_copies[0].wait_recv()
    q_copies[4].start()
    q_copies[1].wait_recv()
    q_copies[5].start()
    own_k.wait()
    own_v.wait()
    for n, device in ((1, zr), (2, zl)):
        k_to(n, kbuf.at[n], device).wait_recv()
        k_to(n + 2, kbuf.at[n], device).start()
    for n, device in ((1, zr), (2, zl)):
        v_to(n, vbuf.at[n], device).wait_recv()
        v_to(n + 2, vbuf.at[n], device).start()
    tab_all = remote(tabv.at[pl.ds(1, 3)], tabv.at[pl.ds(1, 3)], tab_ss, tab_rs, xl)
    tab_all.wait_recv()
    to_smem = pltpu.make_async_copy(tabv, tabs, loc_sem.at[3])
    to_smem.start()
    remote(qfar, qfar, q_ss, q_rs.at[2], xl).wait_recv()
    to_smem.wait()

    eye = lax.broadcasted_iota(jnp.int32, (HD, HD), 0) == lax.broadcasted_iota(
        jnp.int32, (HD, HD), 1
    )

    def pair_at(region, n):
        return pl.ds(region * C + n * PAIR, PAIR)

    homes = {1: (5, xl), 2: (4, xr), 3: (6, xx)}

    def send_back(s, n):
        region, device = homes[s]
        remote(res.at[pair_at(s, n)], res.at[pair_at(region, n)], ret_ss, ret_rs, device).start()

    def form_scores(n, sources):
        owner_z = (z + (1 - 2 * (n % 2)) * ((n + 1) // 2) + ZN) % ZN
        base = (x * ZN + owner_z) * PAIR

        def queries_of(s):
            which = [tabs[s, 0, base + u] for u in range(PAIR)]
            blocks = [qfar[w] if s == 3 else qbuf[s * C + w] for w in which]
            return jnp.concatenate([rows_of(block) for block in blocks], axis=0)

        for k, s in enumerate(sources):
            scores[k] = scores_of(queries_of(s), kbuf[n])

    def settle(n, sources):
        for k, s in enumerate(sources):
            mixed, lse = soften(scores[k], vbuf[n])
            mixed = mixed.astype(BF16)
            for u in range(PAIR):
                here = s * C + n * PAIR + u
                for r in range(R):
                    first = (u * R + r) * L
                    res[here, :, r * HD : (r + 1) * HD] = mixed[first : first + L]
                lsb[here] = jnp.sum(
                    jnp.where(eye, lse[u * HD : (u + 1) * HD], 0.0), axis=0, keepdims=True
                )
            if s:
                send_back(s, n)

    def two_sources(n, sources):
        form_scores(n, sources)
        settle(n, sources)

    def last_halves(buf, send_sem, recv_sems):
        lower, upper = pl.ds(0, P_SIZE // 2), pl.ds(P_SIZE // 2, P_SIZE // 2)
        last = recv_sems.at[ZN - 1]
        return (
            remote(buf.at[5, lower], buf.at[7, lower], send_sem, last, zr),
            remote(buf.at[6, upper], buf.at[7, upper], send_sem, last, zl),
        )

    def step(h, carry):
        @pl.when(h == 3)
        def _():
            remote(qfar, qfar, q_ss, q_rs.at[3], xl).wait_recv()

        @pl.when(h == 4)
        def _():
            for m, device in ((3, zr), (4, zl)):
                k_to(m, kbuf.at[m], device).wait_recv()
                k_to(m + 2, kbuf.at[m], device).start()

        @pl.when(h == 6)
        def _():
            for m, device in ((3, zr), (4, zl)):
                v_to(m, vbuf.at[m], device).wait_recv()
                v_to(m + 2, vbuf.at[m], device).start()

        late_step = jnp.where(h < 3, 0, 1)

        @pl.when(h >= 3)
        def _():
            two_sources(h - 3 * late_step, (3, 0))

        @pl.when((h < 3) | (h >= 6))
        def _():
            two_sources(h - 3 * late_step, (1, 2))

        return carry

    lax.fori_loop(0, ZN, step, 0)

    every = (3, 1, 2, 0)

    def last_step(n, carry):
        @pl.when(n == 5)
        def _():
            k_to(5, kbuf.at[5], zr).wait_recv()
            k_to(6, kbuf.at[6], zl).wait_recv()
            for copy in last_halves(kbuf, k_ss, k_rs):
                copy.start()

        @pl.when(n == 7)
        def _():
            k_to(7, kbuf.at[7], zr).wait_recv()

        form_scores(n, every)

        @pl.when(n == 5)
        def _():
            v_to(5, vbuf.at[5], zr).wait_recv()
            v_to(6, vbuf.at[6], zl).wait_recv()
            for copy in last_halves(vbuf, v_ss, v_rs):
                copy.start()

        @pl.when(n == 7)
        def _():
            v_to(7, vbuf.at[7], zr).wait_recv()

        settle(n, every)
        return carry

    lax.fori_loop(5, ZN, last_step, 0)
    lse_copies = [
        remote(lsb.at[pl.ds(1 * C, C)], lsb.at[pl.ds(5 * C, C)], lse_ss, lse_rs, xl),
        remote(lsb.at[pl.ds(2 * C, C)], lsb.at[pl.ds(4 * C, C)], lse_ss, lse_rs, xr),
        remote(lsb.at[pl.ds(3 * C, C)], lsb.at[pl.ds(6 * C, C)], lse_ss, lse_rs, xx),
    ]
    for copy in lse_copies:
        copy.start()

    came = pl.ds(4 * C, 3 * C)
    res_all = remote(res.at[came], res.at[came], ret_ss, ret_rs, xl)
    lse_all = remote(lsb.at[came], lsb.at[came], lse_ss, lse_rs, xl)
    res_all.wait_recv()
    lse_all.wait_recv()

    def attn_copy(g, k):
        quarter = pl.ds(g * 4, 4)
        return remote(
            attn.at[quarter], attn_sib.at[quarter], att_ss, att_rs.at[(k + 2) // 3], sibling
        )

    def merge(k, carry):
        g = (y + jnp.where(k == 0, 2, jnp.where(k == 1, 1, jnp.where(k == 2, 3, 0)))) % YN
        for e in range(4):
            c = g * 4 + e
            where = slot_s[c]
            prefix = rows_of(res[where]).astype(F32)
            prefix_lse = jnp.sum(jnp.where(eye, lsb[where], 0.0), axis=1, keepdims=True)
            suffix_lse = sfl[c]
            largest = jnp.maximum(prefix_lse, suffix_lse)
            a = jnp.exp(prefix_lse - largest)
            b = jnp.exp(suffix_lse - largest)
            joined = ((a * prefix + b * sfo[c]) / (a + b)).astype(BF16)
            for r in range(R):
                attn[c, :, r * HD : (r + 1) * HD] = joined[r * L : (r + 1) * L]
        attn_copy(g, k).start()
        return carry

    lax.fori_loop(0, C // 4, merge, 0)

    squares[...] = jnp.zeros_like(squares)
    dots[...] = jnp.zeros_like(dots)

    def far_copies(i):
        return (
            remote(part.at[i, far_at, 0], far.at[i, 0], far_ss, far_rs.at[i], yr_same),
            remote(part.at[i, far_at, 1], far.at[i, 1], far_ss, far_rs.at[i], yl_same),
        )

    def now_copies(i):
        return (
            remote(part.at[i, yr_at, 1], near.at[i, core], now_ss, near_rs.at[i], yr[1]),
            remote(part.at[i, yl_at, 0], near.at[i, 2 + core], now_ss, near_rs.at[i], yl[0]),
        )

    def late_copies(i):
        return (
            remote(part.at[i, yr_at, 0], near.at[i, core], late_ss, near_rs.at[i], yr[0]),
            remote(part.at[i, yl_at, 1], near.at[i, 2 + core], late_ss, near_rs.at[i], yl[1]),
        )

    def sib_copy(i):
        return remote(part.at[i, y, 1 - core], near.at[i, 4], sib_ss, near_rs.at[i], sibling)

    def product(i, chunks):
        def rows(ref):
            blocks = [ref[pl.ds(g * 4, 4)].reshape(4 * L, R * HD) for g in chunks]
            return jnp.concatenate(blocks, axis=0)

        summed = jnp.dot(rows(attn), wbuf[0, i], preferred_element_type=F32) + jnp.dot(
            rows(attn_sib), wbuf[1, i], preferred_element_type=F32
        )
        for e, g in enumerate(chunks):
            block = summed[e * 4 * L : (e + 1) * 4 * L].astype(BF16)
            part[i, g] = block.reshape(2, ROWS, TILE)

    def multiply_far(i):
        product(i, (far_at,))
        for copy in far_copies(i):
            copy.start()

    def multiply_rest(i):
        product(i, (yr_at, yl_at, y))
        for copy in now_copies(i) + (sib_copy(i),):
            copy.start()

    def pass_on(i):
        late_r, late_l = late_copies(i)
        remote(far.at[i], far.at[i], far_ss, far_rs.at[i], yr_same).wait_recv()
        part[i, yr_at, 0] = (part[i, yr_at, 0].astype(F32) + far[i, 0].astype(F32)).astype(BF16)
        late_r.start()
        part[i, yl_at, 1] = (part[i, yl_at, 1].astype(F32) + far[i, 1].astype(F32)).astype(BF16)
        late_l.start()

    token = lax.broadcasted_iota(jnp.int32, (ROWS, 1), 0)
    first_cand = t * 2
    live = (token % L) < jnp.where(token < L, len_s[first_cand], len_s[first_cand + 1])

    def finish(i):
        remote(near.at[i], near.at[i], now_ss, near_rs.at[i], yr_same).wait_recv()
        for side, kept in ((core, part[i, y, core]), (1 - core, near[i, 4])):
            columns = pl.ds(pl.multiple_of(side * (D // 2) + i * TILE, TILE), TILE)
            total = (
                residual[:, columns].astype(F32)
                + kept.astype(F32)
                + near[i, side].astype(F32)
                + near[i, 2 + side].astype(F32)
            )
            out = jnp.where(live, total, 0.0).astype(BF16)
            hidden[:, columns] = out
            v = out.astype(F32)
            sq = v * v
            pr = v * head_w[:, columns]
            squares[...] += functools.reduce(
                jnp.add, [sq[:, k * 128 : (k + 1) * 128] for k in range(TILE // 128)]
            )
            dots[...] += functools.reduce(
                jnp.add, [pr[:, k * 128 : (k + 1) * 128] for k in range(TILE // 128)]
            )

    pltpu.make_async_copy(wbuf.at[0], wbuf.at[0], w_sem).wait()
    w_all = remote(wbuf.at[1], wbuf.at[1], ws_ss, ws_rs, sibling)
    w_all.wait_recv()
    attn_all = remote(attn, attn_sib, att_ss, att_rs.at[0], sibling)
    attn_rest = remote(attn.at[pl.ds(0, 12)], attn_sib.at[pl.ds(0, 12)], att_ss, att_rs.at[1], sibling)
    attn_copy(far_at, 0).wait_recv()
    res_copy.wait()
    head_copy.wait()

    def all_sent():
        others = pl.ds(1, ZN - 1)
        for copy in (
            remote(kbuf.at[others], kbuf.at[others], k_ss, k_rs.at[0], zr),
            remote(vbuf.at[others], vbuf.at[others], v_ss, v_rs.at[0], zr),
            remote(qbuf, qbuf, q_ss, q_rs.at[0], xr),
            tab_all, res_all, lse_all, w_all, attn_all,
        ):
            copy.wait_send()

    def tile_step(i, carry):
        @pl.when(i < TILES)
        def _():
            multiply_far(i)

        @pl.when(i == TILES)
        def _():
            all_sent()

        @pl.when(i == 1)
        def _():
            attn_rest.wait_recv()

        @pl.when((i >= 1) & (i < TILES + 1))
        def _():
            multiply_rest(i - 1)

        @pl.when((i >= AHEAD) & (i < TILES + AHEAD))
        def _():
            pass_on(i - AHEAD)

        @pl.when(i >= BEHIND)
        def _():
            finish(i - BEHIND)

        return carry

    lax.fori_loop(0, TILES + BEHIND, tile_step, 0)
    tiles = near.at[:, pl.ds(0, 2)]
    for sem in (far_ss, now_ss, late_ss):
        remote(tiles, tiles, sem, near_rs.at[0], yr_same).wait_send()
    remote(far.at[:, 0], far.at[:, 0], sib_ss, near_rs.at[0], sibling).wait_send()

    mean = jnp.sum(squares[...], axis=1, keepdims=True) * (1.0 / D)
    logit = jnp.sum(dots[...], axis=1, keepdims=True) * lax.rsqrt(mean + 1e-06)
    reward = 1.0 / (1.0 + jnp.exp(-logit))
    lane_row = lax.broadcasted_iota(jnp.int32, (1, 128), 1)
    for a in range(2):
        wanted = jnp.full((1, 128), -1, jnp.int32)
        for k in range(4):
            wanted = jnp.where(lane_row == k, a * L + mark_s[k, first_cand + a], wanted)
        picked = jnp.sum(jnp.where(token == wanted, reward, 0.0), axis=0, keepdims=True)
        rewards[a : a + 1, :] = picked[:, :4]


def fused(group, lens, marks, q, ck, cv, pk, pv, residual, weight, head_w):
    dma = pltpu.SemaphoreType.DMA
    any_space = pl.BlockSpec(memory_space=pl.ANY)
    vmem = pl.BlockSpec(memory_space=pltpu.VMEM)
    smem = pl.BlockSpec(memory_space=pltpu.SMEM)
    return pl.pallas_call(
        fused_kernel,
        out_shape=(
            pltpu.VMEM((ROWS, D), BF16),
            pltpu.VMEM((2, 4), F32),
        ),
        in_specs=[smem] * 3 + [any_space] * 8,
        out_specs=(vmem, vmem),
        scratch_shapes=[
            pltpu.VMEM((3 * C, L, R * HD), BF16),
            pltpu.VMEM((C, L, R * HD), BF16),
            pltpu.VMEM((C * L, HD), BF16),
            pltpu.VMEM((C * L, HD), BF16),
            pltpu.VMEM((ZN, P_SIZE, HD), BF16),
            pltpu.VMEM((ZN, P_SIZE, HD), BF16),
            pltpu.VMEM((XN, 8, 128), jnp.int32),
            pltpu.SMEM((XN, 8, 128), jnp.int32),
            pltpu.VMEM((7 * C, L, R * HD), BF16),
            pltpu.VMEM((7 * C, 1, HD), F32),
            pltpu.VMEM((C, R * L, HD), F32),
            pltpu.VMEM((C, R * L, HD), F32),
            pltpu.SMEM((C,), jnp.int32),
            pltpu.VMEM((XN, PAIR * R * L, P_SIZE), F32),
            pltpu.VMEM((C, L, R * HD), BF16),
            pltpu.VMEM((C, L, R * HD), BF16),
            pltpu.VMEM((2, TILES, R * HD, TILE), BF16),
            pltpu.VMEM((TILES, YN, 2, ROWS, TILE), BF16),
            pltpu.VMEM((TILES, 2, ROWS, TILE), BF16),
            pltpu.VMEM((TILES, 5, ROWS, TILE), BF16),
            pltpu.VMEM((ROWS, D), BF16),
            pltpu.VMEM((1, D), F32),
            pltpu.VMEM((ROWS, 128), F32),
            pltpu.VMEM((ROWS, 128), F32),
            dma((8,)), dma, dma, dma, dma((4,)), dma, dma((ZN,)), dma, dma((ZN,)),
            dma, dma, dma, dma,
            dma, dma, dma, dma, dma((2,)), dma, dma((TILES,)), dma, dma, dma, dma((TILES,)),
        ],
        compiler_params=pltpu.CompilerParams(
            collective_id=0, has_side_effects=True, vmem_limit_bytes=VMEM_LIMIT
        ),
        cost_estimate=pl.CostEstimate(
            flops=2 * 2 * 64 * 128 * P_SIZE * HD + 2 * C * L * R * HD * D,
            bytes_accessed=16 << 20,
            transcendentals=8 << 20,
        ),
    )(group, lens, marks, q, ck, cv, pk, pv, residual, weight, head_w)


def local(
    cand_q, cand_k, cand_v, prompt_k, prompt_v, cand_group, cand_len, boundaries,
    residual, out_weight, head_weight,
):
    hidden, rewards = fused(
        cand_group,
        cand_len,
        boundaries.T,
        cand_q.reshape(C, L, R * HD),
        cand_k,
        cand_v,
        prompt_k,
        prompt_v,
        residual,
        out_weight,
        head_weight.reshape(1, D),
    )
    return hidden, rewards


def solution(mesh):
    in_specs = (
        P("dp", "tensor"),
        P("dp", "tensor"),
        P("dp", "tensor"),
        P("dp", "tensor"),
        P("dp", "tensor"),
        P("dp"),
        P("dp"),
        P("dp", None),
        P(("dp", "tensor"), None),
        P("tensor", None),
        P(),
    )
    out_specs = (P(("dp", "tensor"), None), P(("dp", "tensor"), None))
    return jax.shard_map(local, mesh=mesh, in_specs=in_specs, out_specs=out_specs, check_vma=False)
```
